512 devices in a mesh: tp: 8 (over x, core), dp: 64 (over z, y).
Axes of the slice: x: 4, y: 4, z: 16, core: 2. Of those that a mesh axis runs over, the one named last changes fastest.
Arguments:
- queries: bfloat16 [256, 128, 576], P('dp'), may hold values from -30 to 30
- lengths: int32 [256], P('dp'), may hold values from 2 to 1024, as said below
- resident_pages: bfloat16 [2048, 64, 576], P('dp', 'tp'), may hold values from -3 to 3
- resident_scale: bfloat16 [2048], P('dp'), may hold values from 0.69921875 to 1.34375
- prefill_written_pages: bfloat16 [2048, 64, 576], P('dp', 'tp'), may hold values from -3 to 3
- prefill_scale: bfloat16 [2048], P('dp'), may hold values from 0.69921875 to 1.34375
- page_slot: int32 [2048], P('dp'), may hold values from 0 to 2047, as said below
- tokens: bfloat16 [1024, 7168], P('dp'), may hold values from -3 to 3
- expert_ids: int32 [1024, 8], P('dp'), may hold values from 0 to 31, all different within a row; in each aligned block of 16 rows (0 to 15, 16 to 31, ...) at most 8 rows name the same one
- gate_weights: bfloat16 [1024, 8], P('dp'), may hold values from 0.079589844 to 0.29882812
- gate_projection: bfloat16 [64, 7168, 512], P('dp', 'tp'), may hold values from -0.0625 to 0.0625
- up_weights: bfloat16 [64, 7168, 512], P('dp', 'tp'), may hold values from -0.0625 to 0.0625
- down_weights: bfloat16 [64, 512, 7168], P('dp', None, 'tp'), may hold values from -0.1875 to 0.1875
Outputs:
- attention_out: bfloat16 [256, 128, 512], P('dp', 'tp')
- moe_out: bfloat16 [1024, 7168], P('dp', 'tp')
The draws below stay inside these ranges and needn't reach their ends.
Inputs may be any that keep to these rules, and one draw needn't show every extreme that they name: `page_slot`: A permutation of the slots. Slot s is position s % 32 of dp index s // 32. Of the pages held by one dp index at most 1 go to any one dp index, and every dp index sends its pages with the same multiset of offsets (target index minus own index, modulo 64). `lengths`: some request has exactly 1024. `expert_ids`: of the rows of one dp index, at most 8 name any one expert.
All inputs are finite; a program needn't handle non-finite values.
Results may differ from the reference program's by a relative error of at most 0.0065.
Values may be sent and summed in bfloat16 or wider, within the bound.
A program may use at most 64 MiB of HBM per device.

```python
import math
import jax
import jax.numpy as jnp
import numpy as np
from jax import lax

D = 7168
ATTENTION_HEADS = 128
LATENT_WIDTH = 512
ROTARY_WIDTH = 64
TOP = 8
EXP_FF = 1024
PAGE_TOKENS = 64
REQ_KIND = 2
PG_REQ = 16
TOK_DP = 16
EXPERTS = 32
CAP = 8
TOKENS = 1024
REQUEST_COUNT = 256
CTX = 1024
PG_SRC = 32
PREFILL_COUNT = 2048
RESIDENT_COUNT = 2048
PG_MOST = 1
N_DP = 64


def draw_queries(key, part):
    key = jax.random.fold_in(key, 5)
    value_rows = jnp.clip(jax.random.normal(key, (REQUEST_COUNT, ATTENTION_HEADS, LATENT_WIDTH + ROTARY_WIDTH), jnp.float32), -3.0, 3.0)
    return value_rows.astype(jnp.bfloat16)


def draw_resident_pages(key, part):
    key = jax.random.fold_in(key, 7)
    value_rows = jnp.clip(jax.random.normal(key, (RESIDENT_COUNT, PAGE_TOKENS, LATENT_WIDTH + ROTARY_WIDTH), jnp.float32), -3.0, 3.0)
    return value_rows.astype(jnp.bfloat16)


def draw_lengths(key, part):
    key = jax.random.fold_in(key, 13)
    length_key, chosen_key = jax.random.split(key)
    drawn = jax.random.randint(length_key, (REQUEST_COUNT,), 2, CTX + 1)
    chosen = jax.random.randint(chosen_key, (), 0, REQUEST_COUNT)
    return jnp.where(jnp.arange(REQUEST_COUNT) == chosen, CTX, drawn).astype(jnp.int32)


def draw_page_slot(key, part):
    key = jax.random.fold_in(key, 17)
    offset_key, shuffle_key, order_key = jax.random.split(key, 3)
    pool_size = N_DP * PG_MOST
    offset_pool = jnp.tile(jnp.arange(N_DP), PG_MOST)
    pool_index = jnp.arange(pool_size)
    forced = (pool_index < N_DP) & ((offset_pool == 1) | (offset_pool == N_DP - 1) | (offset_pool == N_DP // 2))
    priority = jax.random.permutation(offset_key, pool_size).astype(jnp.int32) - jnp.where(forced, pool_size, 0).astype(jnp.int32)
    offsets = offset_pool[jnp.argsort(priority, stable=True)][:PG_SRC]
    shuffles = jax.vmap(lambda subkey: jax.random.permutation(subkey, PG_SRC))(jax.random.split(shuffle_key, N_DP))
    target_owner = (jnp.arange(N_DP)[:, None] + offsets[shuffles]) % N_DP
    flattened = target_owner.reshape(-1)
    onehot = (flattened[:, None] == jnp.arange(N_DP)[None, :]).astype(jnp.int32)
    ranking = jnp.sum((jnp.cumsum(onehot, axis=0) - onehot) * onehot, axis=1)
    orders = jax.vmap(lambda subkey: jax.random.permutation(subkey, PG_SRC))(jax.random.split(order_key, N_DP))
    position = orders[flattened, ranking]
    return (flattened * PG_SRC + position).astype(jnp.int32)


def shard_levels(key, dims, cuts, smallest, top_value):
    gain, own = 1.0, jax.random.fold_in(key, 6)
    for dim, blocks in cuts:
        steps = jnp.exp(jax.random.uniform(jax.random.fold_in(own, dim), (blocks,), jnp.float32, smallest / len(cuts), top_value / len(cuts)))
        gain = gain * jnp.repeat(steps, dims[dim] // blocks).reshape([-1 if axis == dim else 1 for axis in range(len(dims))])
    return gain


def routed_block(rng, own, number, rows, amount, top, reach, lean):
    order = jax.random.permutation(rng, amount)
    packed, usual = portions_of(amount, rows * top, reach, lean, True), portions_of(amount, rows * top, reach, lean, False)
    places = jnp.arange(amount)

    def named(tallies, rotation):
        used = int((tallies > 0).sum())
        fixed = max(1, used // 4)
        passed = fixed + (places - fixed + rotation * (used - fixed)) % max(1, amount - fixed)
        return jnp.zeros((amount,), jnp.int32).at[order[jnp.where(places < fixed, places, passed)]].set(jnp.asarray(tallies, jnp.int32))

    tallies = jnp.where(number % 4 == 0, named(packed, number // 4), named(usual, number - number // 4 - 1))
    mixed = jax.random.permutation(jax.random.fold_in(own, 3), amount)
    donor, sink = mixed[0:amount // 2 * 2:2], mixed[1:amount // 2 * 2:2]
    margin = jnp.minimum(tallies[donor] - 1, reach - tallies[sink]) // 2
    margin = jnp.where((donor == order[0]) | (sink == order[0]) | (tallies[sink] == 0), 0, jnp.maximum(margin, 0))
    passed = jax.random.randint(jax.random.fold_in(own, 4), (amount // 2,), 0, 1 << 20) % (margin + 1)
    tallies = tallies.at[donor].add(-passed).at[sink].add(passed)
    items = jnp.searchsorted(jnp.cumsum(tallies), jnp.arange(rows * top), side="right").astype(jnp.int32)
    grid = items.reshape(top, rows).T
    grid = grid[jax.random.permutation(jax.random.fold_in(own, 1), rows)]
    rotation = jax.random.randint(jax.random.fold_in(own, 2), (rows, 1), 0, top)
    return jnp.take_along_axis(grid, (jnp.arange(top)[None, :] + rotation) % top, axis=1)


def portions_of(count, total, bound, slope, full):
    portions = [(1 << 20) // math.isqrt(rank ** slope) + 1 for rank in range(1, count + 1)]
    largest = bound if full else min(bound, max(-(-total // count), total * portions[0] // sum(portions)))
    least = 1 if total - largest >= count - 1 else 0
    holding, rest = [largest] + [least] * (count - 1), total - largest - least * (count - 1)
    while rest > 0:
        movable = [i for i in range(1, count) if holding[i] < largest] or [i for i in range(1, count) if holding[i] < bound]
        pool, budget = sum([portions[i] for i in movable]), rest
        for i in movable:
            addition = min(bound - holding[i], max(1, budget * portions[i] // pool), rest)
            holding[i] = holding[i] + addition
            rest = rest - addition
    return np.array(holding)


def bell_draw(key, extent, spread, reach, cuts=(), kind=jnp.bfloat16):
    entries = spread * jax.random.normal(key, extent, jnp.float32)
    if cuts:
        entries = entries * shard_levels(key, extent, cuts, -0.22, 0.18)
    return jnp.clip(entries, -reach, reach).astype(kind)


def setup_inputs(seed: int = 0) -> dict:
    keys = jax.random.split(jax.random.key(seed), 14)
    queries = draw_queries(jax.random.fold_in(keys[13], 71), 0)
    lengths = draw_lengths(jax.random.fold_in(keys[13], 71), 0)
    resident_pages = draw_resident_pages(jax.random.fold_in(keys[13], 71), 0)
    resident_scale = jnp.clip(jnp.exp(math.log(1.34375) - 0.6532559 * jax.random.uniform(keys[3], (RESIDENT_COUNT,), jnp.float32) ** shard_levels(keys[3], (RESIDENT_COUNT,), ((0, 64),), -0.2, 0.2)), 0.69921875, 1.34375).astype(jnp.bfloat16)
    prefill_written_pages = bell_draw(keys[4], (PREFILL_COUNT, PAGE_TOKENS, LATENT_WIDTH + ROTARY_WIDTH), 1.0, 3.0, ((0, 64), (1, 8)))
    prefill_scale = jnp.clip(jnp.exp(math.log(1.34375) - 0.6532559 * jax.random.uniform(keys[5], (PREFILL_COUNT,), jnp.float32) ** shard_levels(keys[5], (PREFILL_COUNT,), ((0, 64),), -0.2, 0.2)), 0.69921875, 1.34375).astype(jnp.bfloat16)
    page_slot = draw_page_slot(jax.random.fold_in(keys[13], 71), 0)
    tokens = bell_draw(keys[7], (TOKENS, D), 1.0, 3.0, ((0, 64),))
    expert_ids_keys = jax.random.split(jax.random.fold_in(keys[8], 1), TOKENS // TOK_DP)
    expert_ids_turns = jax.random.permutation(jax.random.fold_in(keys[8], 3), TOKENS // TOK_DP)
    expert_ids = jax.vmap(lambda own, number: routed_block(jax.random.fold_in(keys[8], 2), own, number, TOK_DP, EXPERTS, TOP, CAP, 2))(expert_ids_keys, expert_ids_turns).reshape((TOKENS, TOP))
    gate_weights = jnp.clip(0.079589844 + 0.21923828 * jax.random.uniform(keys[9], (TOKENS, TOP), jnp.float32) ** shard_levels(keys[9], (TOKENS, TOP), ((0, 64),), -0.2, 0.2), 0.079589844, 0.29882812).astype(jnp.bfloat16)
    gate_projection = bell_draw(keys[10], (N_DP, D, EXP_FF // 2), D ** -0.5, 0.0625, ((0, 64), (1, 8)))
    up_weights = bell_draw(keys[11], (N_DP, D, EXP_FF // 2), D ** -0.5, 0.0625, ((0, 64), (1, 8)))
    down_weights = bell_draw(keys[12], (N_DP, EXP_FF // 2, D), EXP_FF ** -0.5, 0.1875, ((0, 64), (2, 8)))
    return dict(queries=queries, lengths=lengths, resident_pages=resident_pages, resident_scale=resident_scale, prefill_written_pages=prefill_written_pages, prefill_scale=prefill_scale, page_slot=page_slot, tokens=tokens, expert_ids=expert_ids, gate_weights=gate_weights, gate_projection=gate_projection, up_weights=up_weights, down_weights=down_weights)


softmax_factor = 192.0 ** -0.5


def attend_one(queried, latent_rows, scales, length):
    scores = jnp.dot(queried, latent_rows.T, preferred_element_type=jnp.float32) * (scales * softmax_factor)[None, :]
    visible = (jnp.arange(latent_rows.shape[0]) < length)[None, :]
    highest = jnp.max(jnp.where(visible, scores, -1e30), axis=1, keepdims=True)
    expos = jnp.exp(jnp.where(visible, scores - highest, -1e30))
    denominator = jnp.sum(expos, axis=1, keepdims=True)
    weight_rows = (expos * scales[None, :]).astype(jnp.bfloat16)
    summed_rows = jnp.dot(weight_rows, latent_rows[:, :LATENT_WIDTH], preferred_element_type=jnp.float32)
    return (summed_rows / denominator).astype(jnp.bfloat16)


def reference(queries, lengths, resident_pages, resident_scale, prefill_written_pages, prefill_scale, page_slot, tokens, expert_ids, gate_weights, gate_projection, up_weights, down_weights):
    key_value_width = LATENT_WIDTH + ROTARY_WIDTH
    placed = jnp.zeros_like(prefill_written_pages).at[page_slot].set(prefill_written_pages)
    placed_scale = jnp.zeros_like(prefill_scale).at[page_slot].set(prefill_scale)
    resident = resident_pages.reshape(N_DP, REQ_KIND, CTX, key_value_width)
    arrived = placed.reshape(N_DP, REQ_KIND, CTX, key_value_width)
    caches = jnp.concatenate([resident, arrived], axis=1).reshape(REQUEST_COUNT, CTX, key_value_width)
    page_scales = jnp.concatenate([resident_scale.reshape(N_DP, REQ_KIND, PG_REQ), placed_scale.reshape(N_DP, REQ_KIND, PG_REQ)], axis=1)
    token_scales = jnp.repeat(page_scales.reshape(REQUEST_COUNT, PG_REQ).astype(jnp.float32), PAGE_TOKENS, axis=1)
    attention_out = lax.map(lambda request_items: attend_one(*request_items), (queries, caches, token_scales, lengths))

    def expert_step(running, expert):
        chosen = expert_ids == expert
        member = jnp.sum(chosen.astype(jnp.int32), axis=1)
        gating = jnp.sum(jnp.where(chosen, gate_weights.astype(jnp.float32), 0.0), axis=1)
        ordering = jnp.argsort(1 - member, stable=True)[: N_DP * CAP].astype(jnp.int32)
        token_rows = tokens[ordering]
        combined = jnp.zeros((N_DP * CAP, D), jnp.float32)
        for half in range(2):
            index = (2 * expert + half).astype(jnp.int32)
            gate_half = lax.dynamic_index_in_dim(gate_projection, index, 0, keepdims=False)
            up_half = lax.dynamic_index_in_dim(up_weights, index, 0, keepdims=False)
            down_half = lax.dynamic_index_in_dim(down_weights, index, 0, keepdims=False)
            gate_sum = jnp.dot(token_rows, gate_half, preferred_element_type=jnp.float32)
            up_sum = jnp.dot(token_rows, up_half, preferred_element_type=jnp.float32)
            hidden = (jax.nn.silu(gate_sum) * up_sum).astype(jnp.bfloat16)
            part = jnp.dot(hidden, down_half, preferred_element_type=jnp.float32).astype(jnp.bfloat16)
            combined = combined + part.astype(jnp.float32)
        running = running.at[ordering].add(gating[ordering][:, None] * combined)
        return running, None

    running, unused = lax.scan(expert_step, jnp.zeros((TOKENS, D), jnp.float32), jnp.arange(EXPERTS, dtype=jnp.int32))
    return attention_out, running.astype(jnp.bfloat16)
```

```python
import jax
import jax.numpy as jnp
from jax import lax
from jax.experimental import pallas as pl
from jax.experimental.pallas import tpu as pltpu
from jax.sharding import PartitionSpec as P

F32, BF16, I32 = jnp.float32, jnp.bfloat16, jnp.int32
MESH = pl.DeviceIdType.MESH
FACTOR = 192.0 ** (-0.5)
MASKED = -1e30
NZ, NY, NX = 16, 4, 4
QN = 4
WD = 896
ORDER = [0, 15, 1, 14, 2, 13, 3, 12, 4, 11, 5, 10, 6, 9, 7, 8]
PLACE = {rel: k for k, rel in enumerate(ORDER)}


def dot(a, b, ca=1, cb=0):
    return lax.dot_general(a, b, (((ca,), (cb,)), ((), ())), preferred_element_type=F32)


def iota(shape, dim):
    return lax.broadcasted_iota(I32, shape, dim)


def kernel(
    queries, lengths, resident, resident_scale, pages, prefill_scale, page_slot,
    tokens, ids, gates, gate_w, up_w, down_w,
    att_out, moe_out,
    v_gate, v_up, v_down, zbuf, dsend, ffn_x, gu, core_send, core_recv, x_send, x_recv,
    h_all, r_buf, p_buf, zs, zr, own_sum,
    page_tail, pg_send, pg_recv, pg_turn, pg_slots, new_k, scores, ml_all, at_send, at_recv,
    load_sem, tok_sem, ring_s, ring_r, yd_s, yd_r, co_s, co_r, xx_s, xx_r, hh_s, hh_r,
    yr_s, yr_r, zr_s, zr_r, pz_s, pz_r, py_s, py_r, ml_s, ml_r, at_s, at_r,
):
    tp = lax.axis_index("tp")
    dp = lax.axis_index("dp")
    x, c = tp // 2, tp % 2
    z, y = dp // NY, dp % NY

    def at_dp(zz, yy):
        return {"dp": zz * NY + yy}

    def z_peer(d):
        return at_dp(lax.rem(z + d, NZ), y)

    def y_peer(d):
        return lax.rem(y + d, NY)

    def tp_peer(d):
        return lax.rem(tp + d, 8)

    def x_peer(d):
        return lax.rem(x + d, NX)

    sibling = x * 2 + (1 - c)

    def rows(ref, start, size):
        if not isinstance(start, int):
            start = pl.multiple_of(start, 8 if size % 16 else 16)
        return ref.at[pl.ds(start, size), :]

    started = []

    def remote(src, dst, ssem, rsem, where):
        return pltpu.make_async_remote_copy(
            src_ref=src, dst_ref=dst, send_sem=ssem, recv_sem=rsem,
            device_id=where, device_id_type=MESH,
        )

    def send(src, dst, ssem, rsem, where):
        copy = remote(src, dst, ssem, rsem, where)
        copy.start()
        started.append(copy)

    def arrive(dst, rsem, ssem, where):
        remote(dst, dst, ssem, rsem, where).wait_recv()

    tok_copy = pltpu.make_async_copy(
        tokens.at[:, pl.ds(pl.multiple_of(tp * WD, 128), WD)], zbuf.at[pl.ds(0, 16), pl.ds(0, WD)], tok_sem
    )
    tok_copy.start()
    loads = [
        pltpu.make_async_copy(gate_w, v_gate, load_sem.at[0]),
        pltpu.make_async_copy(up_w, v_up, load_sem.at[1]),
        pltpu.make_async_copy(down_w, v_down, load_sem.at[2]),
    ]
    for copy in loads:
        copy.start()

    barrier = pltpu.get_barrier_semaphore()
    for d in range(1, NZ):
        pl.semaphore_signal(barrier, inc=1, device_id=z_peer(d), device_id_type=MESH)
    for d in range(1, NY):
        pl.semaphore_signal(barrier, inc=1, device_id=at_dp(z, y_peer(d)), device_id_type=MESH)
    for d in range(1, 8):
        pl.semaphore_signal(barrier, inc=1, device_id={"tp": tp_peer(d)}, device_id_type=MESH)

    lane = iota((16, 128), 1)
    idv = ids[...]
    gwv = gates[...].astype(F32)
    chosen = jnp.zeros((16, 128), F32)
    gate_l = jnp.zeros((16, 128), F32)
    for k in range(8):
        chosen += jnp.where(idv[:, k : k + 1] == lane, 1.0, 0.0)
        gate_l += jnp.where(idv[:, k : k + 1] + 32 == lane, gwv[:, k : k + 1], 0.0)
    before = (iota((16, 16), 1) < iota((16, 16), 0)).astype(BF16)
    rank = dot(before, chosen.astype(BF16))
    zbuf[0:16, WD:1024] = (chosen * (rank + 1.0) + gate_l).astype(BF16)
    tok_copy.wait()
    pl.semaphore_wait(barrier, NZ - 1 + NY - 1 + 7)

    def ring(s):
        right = (NZ - s) % NZ
        send(
            rows(zbuf, 16 * PLACE[right], 16), rows(zbuf, 16 * PLACE[right - 1 if right else 15], 16),
            ring_s.at[right - 1 if right else 15], ring_r.at[right - 1 if right else 15], z_peer(1),
        )
        if s < 7:
            send(
                rows(zbuf, 16 * PLACE[s], 16), rows(zbuf, 16 * PLACE[s + 1], 16),
                ring_s.at[s + 1], ring_r.at[s + 1], z_peer(NZ - 1),
            )

    def ring_wait(s):
        got = NZ - 1 - s
        arrive(rows(zbuf, 16 * PLACE[got], 16), ring_r.at[got], ring_s.at[got], z_peer(1))
        if s < 7:
            arrive(rows(zbuf, 16 * PLACE[s + 1], 16), ring_r.at[s + 1], ring_s.at[s + 1], z_peer(NZ - 1))

    e0 = 2 * z

    def dispatch(q):
        meta = zbuf[64 * q : 64 * q + 64, WD:1024]
        pick = (iota((16, 128), 1) == e0 + iota((16, 128), 0)).astype(BF16)
        slots = dot(pick, meta, 1, 1).astype(I32)
        col = iota((1, 64), 1)
        base = col // 16 * 8 - 1
        t0 = jnp.where(slots[0:1] > 0, slots[0:1] + base, -1)
        t1 = jnp.where(slots[1:2] > 0, slots[1:2] + base + 32, -1)
        row = iota((64, 64), 0)
        g = jnp.where(row == jnp.where(row < 32, t0, t1), 1.0, 0.0).astype(BF16)
        dsend[64 * q : 64 * q + 64, :] = dot(g, zbuf[64 * q : 64 * q + 64, 0:WD]).astype(BF16)
        for d in range(1, NY):
            to = y_peer(d)
            send(
                rows(dsend, 64 * q + to // 2 * 32, 32), rows(ffn_x, 128 * q + y * 32, 32),
                yd_s.at[q, d], yd_r.at[q, d], at_dp(z, to),
            )
        own = dsend[pl.ds(pl.multiple_of(64 * q + y // 2 * 32, 32), 32), :]
        ffn_x[pl.ds(pl.multiple_of(128 * q + y * 32, 32), 32), :] = own

    def first_ffn(q):
        if q == 0:
            loads[0].wait()
            loads[1].wait()
        for d in range(1, NY):
            arrive(rows(ffn_x, 128 * q + y_peer(NY - d) * 32, 32), yd_r.at[q, d], yd_s.at[q, d], at_dp(z, y_peer(d)))
        a = ffn_x[128 * q : 128 * q + 128, :]
        gu[128 * q : 128 * q + 128, 0:512] = dot(a, v_gate[...])
        gu[128 * q : 128 * q + 128, 512:1024] = dot(a, v_up[...])
        theirs = gu[pl.ds(pl.multiple_of(128 * q + (1 - c) * 64, 64), 64), :]
        core_send[64 * q : 64 * q + 64, :] = theirs.astype(BF16)
        send(
            rows(core_send, 64 * q, 64), rows(core_recv, 64 * q, 64), co_s.at[q], co_r.at[q], {"tp": sibling}
        )

    def over_x(q):
        arrive(rows(core_recv, 64 * q, 64), co_r.at[q], co_s.at[q], {"tp": sibling})
        mine = gu[pl.ds(pl.multiple_of(128 * q + c * 64, 64), 64), :]
        own_sum[64 * q : 64 * q + 64, :] = mine + core_recv[64 * q : 64 * q + 64, :].astype(F32)
        x_send[64 * q : 64 * q + 64, :] = own_sum[64 * q : 64 * q + 64, :].astype(BF16)
        for d in range(1, NX):
            to = x_peer(d)
            send(
                rows(x_send, 64 * q + to * 16, 16), rows(x_recv, 64 * q + x * 16, 16),
                xx_s.at[q, d], xx_r.at[q, d], {"tp": to * 2 + c},
            )

    def hidden(q):
        for d in range(1, NX):
            arrive(rows(x_recv, 64 * q + x_peer(NX - d) * 16, 16), xx_r.at[q, d], xx_s.at[q, d], {"tp": x_peer(d) * 2 + c})
        total = own_sum[pl.ds(pl.multiple_of(64 * q + x * 16, 16), 16), :]
        for d in range(1, NX):
            total += x_recv[pl.ds(pl.multiple_of(64 * q + x_peer(d) * 16, 16), 16), :].astype(F32)
        gv, uv = total[:, 0:512], total[:, 512:1024]
        hid = gv / (1.0 + jnp.exp(-gv)) * uv
        place = 128 * q + c * 64 + x * 16
        h_all[pl.ds(pl.multiple_of(place, 16), 16), :] = hid.astype(BF16)
        for d in range(1, 8):
            send(
                rows(h_all, place, 16), rows(h_all, place, 16), hh_s.at[q, d], hh_r.at[q, d], {"tp": tp_peer(d)}
            )

    def second_ffn(q):
        if q == 0:
            loads[2].wait()
        for d in range(1, 8):
            src = tp_peer(8 - d)
            arrive(
                rows(h_all, 128 * q + src % 2 * 64 + src // 2 * 16, 16),
                hh_r.at[q, d], hh_s.at[q, d], {"tp": tp_peer(d)},
            )
        r_buf[128 * q : 128 * q + 128, :] = dot(h_all[128 * q : 128 * q + 128, :], v_down[...]).astype(BF16)
        for d in range(1, NY):
            to = y_peer(d)
            send(
                rows(r_buf, 128 * q + to * 32, 32), rows(p_buf, 128 * q + y * 32, 32),
                yr_s.at[q, d], yr_r.at[q, d], at_dp(z, to),
            )
        place = pl.ds(pl.multiple_of(128 * q + y * 32, 32), 32)
        p_buf[place, :] = r_buf[place, :]

    def combine(q):
        for d in range(1, NY):
            arrive(rows(p_buf, 128 * q + y_peer(NY - d) * 32, 32), yr_r.at[q, d], yr_s.at[q, d], at_dp(z, y_peer(d)))
        meta = zbuf[64 * q : 64 * q + 64, WD:1024].astype(F32)
        ln = iota((64, 128), 1)

        def column(at):
            return jnp.sum(jnp.where(ln == at, meta, 0.0), axis=1, keepdims=True)

        base = iota((64, 1), 0) // 16 * 8 - 1
        col = iota((64, 128), 1)
        s0, s1 = column(e0).astype(I32), column(e0 + 1).astype(I32)
        t0 = jnp.where(s0 > 0, s0 + base, -1)
        t1 = jnp.where(s1 > 0, s1 + base, -1)
        g0, g1 = column(e0 + 32), column(e0 + 33)
        target = jnp.where(col < 64, t0, t1)
        gate = jnp.where(col < 64, g0, g1)
        mix = jnp.where(col % 32 == target, gate, 0.0).astype(BF16)
        zs[64 * q : 64 * q + 64, :] = dot(mix, p_buf[128 * q : 128 * q + 128, :]).astype(BF16)
        for k in range(4 * q, 4 * q + 4):
            rel = ORDER[k]
            if rel:
                back = PLACE[NZ - rel]
                send(rows(zs, 16 * k, 16), rows(zr, 16 * back, 16), zr_s.at[back], zr_r.at[back], z_peer(rel))

    def finish_moe():
        total = zs[0:16, :].astype(F32)
        for k in range(1, NZ):
            arrive(rows(zr, 16 * k, 16), zr_r.at[k], zr_s.at[k], z_peer(1))
            total += zr[16 * k : 16 * k + 16, :].astype(F32)
        moe_out[...] = total.astype(BF16)

    def expand(vector):
        spread = (iota((256, 32), 0) // 8 == iota((256, 32), 1)).astype(BF16)
        return dot(spread, vector, 1, 1)

    def pack_pages():
        slot = page_slot[...]
        target, position = slot // 32, slot % 32
        r16 = iota((64, 32), 0)
        sel = jnp.where(r16 == 0, (position + 1).astype(F32), jnp.where(r16 == 1, prefill_scale[...].astype(F32), 0.0))
        page_tail[:, 0:64] = pages[:, 512:576]
        page_tail[:, 64:128] = expand(sel.astype(BF16)).astype(BF16)
        spread = (iota((32, 256), 1) // 8 == iota((32, 256), 0)).astype(BF16)
        wide = jnp.broadcast_to(target.astype(F32), (16, 32)).astype(BF16)
        goal = dot(wide, spread)[0:1].astype(I32) * 8 + iota((1, 256), 1) % 8
        put = jnp.where(iota((512, 256), 0) == goal, 1.0, 0.0).astype(BF16)
        pg_send[:, 0:512] = dot(put, pages[:, 0:512]).astype(BF16)
        pg_send[:, 512:640] = dot(put, page_tail[...]).astype(BF16)

    def send_pages():
        for d in range(1, NZ):
            to = lax.rem(z + d, NZ)
            send(rows(pg_send, to * 32, 32), rows(pg_recv, z * 32, 32), pz_s.at[d], pz_r.at[d], z_peer(d))
        place = pl.ds(pl.multiple_of(z * 32, 32), 32)
        pg_recv[place, :] = pg_send[place, :]

    def turn_pages():
        for d in range(1, NZ):
            arrive(rows(pg_recv, lax.rem(z + NZ - d, NZ) * 32, 32), pz_r.at[d], pz_s.at[d], z_peer(d))
        r = iota((512, 512), 0)
        src = r % 128 // 8 * 32 + r // 128 * 8 + r % 8
        turn = jnp.where(iota((512, 512), 1) == src, 1.0, 0.0).astype(BF16)
        pg_turn[...] = dot(turn, pg_recv[...]).astype(BF16)
        for d in range(1, NY):
            to = y_peer(d)
            send(rows(pg_turn, to * 128, 128), rows(pg_slots, y * 128, 128), py_s.at[d], py_r.at[d], at_dp(z, to))
        place = pl.ds(pl.multiple_of(y * 128, 128), 128)
        pg_slots[place, :] = pg_turn[place, :]

    def place_pages():
        for d in range(1, NY):
            arrive(rows(pg_slots, y_peer(NY - d) * 128, 128), py_r.at[d], py_s.at[d], at_dp(z, y_peer(d)))
        pick = (iota((16, 128), 1) == 64).astype(BF16)
        position = dot(pick, pg_slots[:, 512:640], 1, 1)[0:1].astype(I32)
        goal = jnp.where(position > 0, (position - 1) * 8 + iota((1, 512), 1) % 8, -1)
        take = jnp.where(iota((256, 512), 0) == goal, 1.0, 0.0).astype(BF16)
        new_k[...] = dot(take, pg_slots[...]).astype(BF16)

    def score(r):
        if r < 2:
            k0 = resident[128 * r : 128 * r + 128, 0:512]
            k1 = resident[128 * r : 128 * r + 128, 512:576]
            wide = jnp.broadcast_to(resident_scale[...].astype(F32), (16, 32)).astype(BF16)
            spread = (iota((128, 32), 0) // 8 + 16 * r == iota((128, 32), 1)).astype(BF16)
            scale = dot(spread, wide, 1, 1)[:, 0:1]
        else:
            k0 = new_k[128 * r - 256 : 128 * r - 128, 0:512]
            k1 = new_k[128 * r - 256 : 128 * r - 128, 512:576]
            scale = new_k[128 * r - 256 : 128 * r - 128, 512:640].astype(F32)[:, 65:66]
        s = dot(k0, queries[r, :, 0:512], 1, 1) + dot(k1, queries[r, :, 512:576], 1, 1)
        local = iota((128, 128), 0)
        seen = local // 8 * 64 + tp * 8 + local % 8 < lengths[r]
        s = jnp.where(seen, s * (scale * FACTOR), MASKED)
        scores[128 * r : 128 * r + 128, :] = s
        m = jnp.max(s, axis=0, keepdims=True)
        l = jnp.sum(jnp.where(seen, jnp.exp(s - m), 0.0), axis=0, keepdims=True)
        ml_all[pl.ds(pl.multiple_of(tp * 8, 8), 8), :] = jnp.where(
            iota((8, 128), 0) == r, m,
            jnp.where(iota((8, 128), 0) == r + 4, l, ml_all[pl.ds(pl.multiple_of(tp * 8, 8), 8), :]),
        )

    def clear_ml():
        ml_all[pl.ds(pl.multiple_of(tp * 8, 8), 8), :] = jnp.zeros((8, 128), F32)

    def send_ml():
        place = rows(ml_all, tp * 8, 8)
        for d in range(1, 8):
            send(place, place, ml_s.at[d], ml_r.at[d], {"tp": tp_peer(d)})

    def weigh():
        for d in range(1, 8):
            arrive(rows(ml_all, tp_peer(8 - d) * 8, 8), ml_r.at[d], ml_s.at[d], {"tp": tp_peer(d)})
        highest = ml_all[0:4, :]
        for i in range(1, 8):
            highest = jnp.maximum(highest, ml_all[8 * i : 8 * i + 4, :])
        total = jnp.zeros((4, 128), F32)
        for i in range(8):
            total += ml_all[8 * i + 4 : 8 * i + 8, :] * jnp.exp(ml_all[8 * i : 8 * i + 4, :] - highest)
        inverse = 1.0 / total
        for r in range(4):
            s = scores[128 * r : 128 * r + 128, :]
            local = iota((128, 128), 0)
            seen = local // 8 * 64 + tp * 8 + local % 8 < lengths[r]
            if r < 2:
                value = resident[128 * r : 128 * r + 128, 0:512]
                wide = jnp.broadcast_to(resident_scale[...].astype(F32), (16, 32)).astype(BF16)
                spread = (iota((128, 32), 0) // 8 + 16 * r == iota((128, 32), 1)).astype(BF16)
                scale = dot(spread, wide, 1, 1)[:, 0:1]
            else:
                value = new_k[128 * r - 256 : 128 * r - 128, 0:512]
                scale = new_k[128 * r - 256 : 128 * r - 128, 512:640].astype(F32)[:, 65:66]
            w = jnp.where(seen, jnp.exp(s - highest[r : r + 1]), 0.0) * (scale * inverse[r : r + 1])
            part = dot(w.T.astype(BF16), value).astype(BF16)
            for i in range(8):
                at_send[64 * i + 16 * r : 64 * i + 16 * r + 16, :] = part[16 * i : 16 * i + 16, :]
        for d in range(1, 8):
            to = tp_peer(d)
            send(rows(at_send, to * 64, 64), rows(at_recv, tp * 64, 64), at_s.at[d], at_r.at[d], {"tp": to})

    def finish_attention():
        total = at_send[pl.ds(pl.multiple_of(tp * 64, 64), 64), :].astype(F32)
        for d in range(1, 8):
            src = tp_peer(8 - d)
            arrive(rows(at_recv, src * 64, 64), at_r.at[d], at_s.at[d], {"tp": tp_peer(d)})
            total += at_recv[pl.ds(pl.multiple_of(src * 64, 64), 64), :].astype(F32)
        total = total.astype(BF16)
        for r in range(4):
            att_out[r] = total[16 * r : 16 * r + 16, :]

    def both(s):
        ring(s)
        ring_wait(s)

    ring(0)
    pack_pages()
    ring_wait(0)
    both(1)
    dispatch(0)
    both(2)
    both(3)
    dispatch(1)
    both(4)
    both(5)
    dispatch(2)
    both(6)
    ring(7)
    first_ffn(0)
    ring_wait(7)
    dispatch(3)
    send_pages()
    first_ffn(1)
    over_x(0)
    first_ffn(2)
    over_x(1)
    hidden(0)
    first_ffn(3)
    over_x(2)
    hidden(1)
    second_ffn(0)
    over_x(3)
    hidden(2)
    second_ffn(1)
    combine(0)
    hidden(3)
    clear_ml()
    score(0)
    score(1)
    second_ffn(2)
    combine(1)
    second_ffn(3)
    combine(2)
    turn_pages()
    combine(3)
    place_pages()
    score(2)
    score(3)
    send_ml()
    weigh()
    finish_moe()
    finish_attention()
    for copy in started:
        copy.wait_send()


def on_device(
    queries, lengths, resident_pages, resident_scale, prefill_written_pages, prefill_scale,
    page_slot, tokens, expert_ids, gate_weights, gate_projection, up_weights, down_weights,
):
    vmem = pl.BlockSpec(memory_space=pltpu.VMEM)
    smem = pl.BlockSpec(memory_space=pltpu.SMEM)
    hbm = pl.BlockSpec(memory_space=pl.ANY)
    dma = pltpu.SemaphoreType.DMA
    return pl.pallas_call(
        kernel,
        out_shape=(
            jax.ShapeDtypeStruct((4, 16, 512), BF16),
            jax.ShapeDtypeStruct((16, WD), BF16),
        ),
        in_specs=[vmem, smem, vmem, vmem, vmem, vmem, vmem, hbm, vmem, vmem, hbm, hbm, hbm],
        out_specs=(vmem, vmem),
        scratch_shapes=[
            pltpu.VMEM((WD, 512), BF16),
            pltpu.VMEM((WD, 512), BF16),
            pltpu.VMEM((512, WD), BF16),
            pltpu.VMEM((256, 1024), BF16),
            pltpu.VMEM((256, WD), BF16),
            pltpu.VMEM((512, WD), BF16),
            pltpu.VMEM((512, 1024), F32),
            pltpu.VMEM((256, 1024), BF16),
            pltpu.VMEM((256, 1024), BF16),
            pltpu.VMEM((256, 1024), BF16),
            pltpu.VMEM((256, 1024), BF16),
            pltpu.VMEM((512, 512), BF16),
            pltpu.VMEM((512, WD), BF16),
            pltpu.VMEM((512, WD), BF16),
            pltpu.VMEM((256, WD), BF16),
            pltpu.VMEM((256, WD), BF16),
            pltpu.VMEM((256, 1024), F32),
            pltpu.VMEM((256, 128), BF16),
            pltpu.VMEM((512, 640), BF16),
            pltpu.VMEM((512, 640), BF16),
            pltpu.VMEM((512, 640), BF16),
            pltpu.VMEM((512, 640), BF16),
            pltpu.VMEM((256, 640), BF16),
            pltpu.VMEM((512, 128), F32),
            pltpu.VMEM((64, 128), F32),
            pltpu.VMEM((512, 512), BF16),
            pltpu.VMEM((512, 512), BF16),
            dma((3,)),
            dma,
            dma((16,)), dma((16,)),
            dma((QN, 4)), dma((QN, 4)),
            dma((QN,)), dma((QN,)),
            dma((QN, 4)), dma((QN, 4)),
            dma((QN, 8)), dma((QN, 8)),
            dma((QN, 4)), dma((QN, 4)),
            dma((16,)), dma((16,)),
            dma((16,)), dma((16,)),
            dma((4,)), dma((4,)),
            dma((8,)), dma((8,)),
            dma((8,)), dma((8,)),
        ],
        compiler_params=pltpu.CompilerParams(
            collective_id=0, has_side_effects=True, vmem_limit_bytes=48 * 1024 * 1024
        ),
    )(
        queries,
        lengths,
        resident_pages.reshape(256, 576),
        resident_scale.reshape(1, 32),
        prefill_written_pages.reshape(256, 576),
        prefill_scale.reshape(1, 32),
        page_slot.reshape(1, 32),
        tokens,
        expert_ids,
        gate_weights,
        gate_projection.reshape(WD, 512),
        up_weights.reshape(WD, 512),
        down_weights.reshape(512, WD),
    )


def solution(mesh):
    placed = (
        P("dp", None, None), P("dp"), P("dp", "tp", None), P("dp"), P("dp", "tp", None), P("dp"),
        P("dp"), P("dp", None), P("dp", None), P("dp", None), P("dp", "tp", None),
        P("dp", "tp", None), P("dp", None, "tp"),
    )
    return jax.shard_map(
        on_device, mesh=mesh, in_specs=placed, out_specs=(P("dp", "tp", None), P("dp", "tp")),
        check_vma=False,
    )
```

```python
import jax
import jax.numpy as jnp
from jax import lax
from jax.experimental import pallas as pl
from jax.experimental.pallas import tpu as pltpu
from jax.sharding import PartitionSpec as P

F32, BF16, I32 = jnp.float32, jnp.bfloat16, jnp.int32
MESH = pl.DeviceIdType.MESH
FACTOR = 192.0 ** (-0.5)
MASKED = -1e30
SCHEDULE = [
    "pack", "score 0", "score 1", "enter", "far", "send_att 0", "far_wait", "near", "dispatch 0",
    "near_wait 1", "dispatch 1", "first 0", "near_wait 2", "dispatch 2", "over_x 0", "near_wait 3", "dispatch 3",
    "send_pages 0", "send_pages 1", "send_pages 2", "send_pages 3", "first 1", "hidden 0", "over_x 1", "first 2",
    "second 0", "hidden 1", "over_x 2", "first 3", "second 1", "hidden 2", "over_x 3", "combine 0", "second 2",
    "hidden 3", "combine 1", "turn 0", "second 3", "combine 2", "turn 1", "combine 3", "turn 2", "finish_att 0",
    "turn 3", "place", "gather", "score 2", "score 3", "send_att 1", "finish_moe", "finish_att 1",
]
NZ, NY, NX = 16, 4, 4
QN = 4
WD = 896
ORDER = [12, 0, 4, 8, 13, 1, 5, 9, 11, 15, 3, 7, 10, 14, 2, 6]
PAGE_ORDER = [8, 9, 7, 10, 6, 11, 5, 12, 4, 13, 3, 14, 2, 15, 1, 0]


def dot(a, b, ca=1, cb=0):
    return lax.dot_general(a, b, (((ca,), (cb,)), ((), ())), preferred_element_type=F32)


def iota(shape, dim):
    return lax.broadcasted_iota(I32, shape, dim)


def kernel(
    queries, lengths, resident, resident_scale, pages, prefill_scale, page_slot,
    tokens, ids, gates, gate_w, up_w, down_w,
    att_out, moe_out,
    v_gate, v_up, v_down, v_q, v_res, v_pages, zbuf, dsend, ffn_x, gu, core_send, core_recv, x_send, x_recv,
    h_all, r_buf, p_buf, zs0, zs, ra, rb, rc, far_send, far_recv, own_sum,
    page_tail, pg_send, pg_recv, pg_turn, pg_slots, new_k, ml, at_send, at_recv, wcol,
    load_sem, zg_s, zg_r, yd_s, yd_r, co_s, co_r, xx_s, xx_r, hh_s, hh_r,
    yr_s, yr_r, rs_s, rs_r, pz_s, pz_r, py_s, py_r, ml_s, ml_r, at_s, at_r,
):
    tp = lax.axis_index("tp")
    dp = lax.axis_index("dp")
    x, c = tp // 2, tp % 2
    z, y = dp // NY, dp % NY

    def at_dp(zz, yy):
        return {"dp": zz * NY + yy}

    def z_peer(d):
        return at_dp(lax.rem(z + d, NZ), y)

    def y_peer(d):
        return lax.rem(y + d, NY)

    def tp_peer(d):
        return lax.rem(tp + d, 8)

    def x_peer(d):
        return lax.rem(x + d, NX)

    sibling = x * 2 + (1 - c)

    def span(start, size):
        if not isinstance(start, int):
            start = pl.multiple_of(start, 8 if size % 16 else 16)
        return pl.ds(start, size)

    def rows(ref, start, size):
        return ref.at[span(start, size), :]

    started = []

    def remote(src, dst, ssem, rsem, where):
        return pltpu.make_async_remote_copy(
            src_ref=src, dst_ref=dst, send_sem=ssem, recv_sem=rsem,
            device_id=where, device_id_type=MESH,
        )

    def send(src, dst, ssem, rsem, where):
        copy = remote(src, dst, ssem, rsem, where)
        copy.start()
        started.append(copy)

    def arrive(dst, rsem, ssem, where):
        remote(dst, dst, ssem, rsem, where).wait_recv()

    barrier = pltpu.get_barrier_semaphore()
    for d in range(1, NZ):
        pl.semaphore_signal(barrier, inc=1, device_id=z_peer(d), device_id_type=MESH)
    for d in range(1, NY):
        pl.semaphore_signal(barrier, inc=1, device_id=at_dp(z, y_peer(d)), device_id_type=MESH)
    for d in range(1, 8):
        pl.semaphore_signal(barrier, inc=1, device_id={"tp": tp_peer(d)}, device_id_type=MESH)

    local = [
        (tokens.at[:, pl.ds(pl.multiple_of(tp * WD, 128), WD)], zbuf.at[pl.ds(16, 16), pl.ds(0, WD)]),
        (pages, v_pages),
        (resident, v_res),
        (queries, v_q),
        (gate_w, v_gate),
        (up_w, v_up),
        (down_w, v_down),
    ]
    loads = [pltpu.make_async_copy(src, dst, load_sem.at[i]) for i, (src, dst) in enumerate(local)]
    for copy in loads:
        copy.start()

    lane = iota((16, 128), 1)
    idv = ids[...].astype(F32).T.astype(I32)
    gwv = gates[...].astype(F32).T
    chosen = jnp.zeros((16, 128), F32)
    gate_l = jnp.zeros((16, 128), F32)
    for k in range(8):
        chosen += jnp.where(idv[:, k : k + 1] == lane, 1.0, 0.0)
        gate_l += jnp.where(idv[:, k : k + 1] + 32 == lane, gwv[:, k : k + 1], 0.0)
    before = (iota((16, 16), 1) < iota((16, 16), 0)).astype(BF16)
    rank = dot(before, chosen.astype(BF16))
    zbuf[16:32, WD:1024] = (chosen * (rank + 1.0) + gate_l).astype(BF16)

    def enter():
        loads[0].wait()
        pl.semaphore_wait(barrier, NZ - 1 + NY - 1 + 7)

    def far():
        for i, d in enumerate((8, 4, 12)):
            send(rows(zbuf, 16, 16), rows(zbuf, 16 * ORDER.index(NZ - d), 16), zg_s.at[i], zg_r.at[i], z_peer(d))

    def far_wait():
        for i, d in enumerate((8, 4, 12)):
            arrive(rows(zbuf, 16 * ORDER.index(NZ - d), 16), zg_r.at[i], zg_s.at[i], z_peer(d))

    passing = [(NZ - 1, 0, 64, 64, 3), (1, 0, 128, 64, 4), (2, 0, 192, 32, 5), (NZ - 2, 16, 224, 32, 6)]

    def near():
        for d, at, there, size, i in passing:
            send(rows(zbuf, at, size), rows(zbuf, there, size), zg_s.at[i], zg_r.at[i], z_peer(d))

    def near_wait(q):
        for d, at, there, size, i in passing:
            if there // 64 == q:
                arrive(rows(zbuf, there, size), zg_r.at[i], zg_s.at[i], z_peer(d))

    e0 = 2 * z

    def dispatch(q):
        meta = zbuf[64 * q : 64 * q + 64, WD:1024]
        pick = (iota((16, 128), 1) == e0 + iota((16, 128), 0)).astype(BF16)
        slots = dot(pick, meta, 1, 1).astype(I32)
        base = iota((1, 64), 1) // 16 * 8 - 1
        t0 = jnp.where(slots[0:1] > 0, slots[0:1] + base, -1)
        t1 = jnp.where(slots[1:2] > 0, slots[1:2] + base + 32, -1)
        row = iota((64, 64), 0)
        g = jnp.where(row == jnp.where(row < 32, t0, t1), 1.0, 0.0).astype(BF16)
        dsend[64 * q : 64 * q + 64, :] = dot(g, zbuf[64 * q : 64 * q + 64, 0:WD]).astype(BF16)
        for d in (2, 1, 3):
            to = y_peer(d)
            send(
                rows(dsend, 64 * q + to // 2 * 32, 32), rows(ffn_x, 128 * q + y * 32, 32),
                yd_s.at[q, d], yd_r.at[q, d], at_dp(z, to),
            )
        ffn_x[span(128 * q + y * 32, 32), :] = dsend[span(64 * q + y // 2 * 32, 32), :]

    def first_ffn(q):
        if q == 0:
            loads[4].wait()
            loads[5].wait()
        for d in range(1, NY):
            arrive(rows(ffn_x, 128 * q + y_peer(NY - d) * 32, 32), yd_r.at[q, d], yd_s.at[q, d], at_dp(z, y_peer(d)))
        a = ffn_x[128 * q : 128 * q + 128, :]
        gu[128 * q : 128 * q + 128, 0:512] = dot(a, v_gate[...])
        gu[128 * q : 128 * q + 128, 512:1024] = dot(a, v_up[...])
        core_send[64 * q : 64 * q + 64, :] = gu[span(128 * q + (1 - c) * 64, 64), :]
        send(
            rows(core_send, 64 * q, 64), rows(core_recv, 64 * q, 64), co_s.at[q], co_r.at[q], {"tp": sibling}
        )

    def over_x(q):
        arrive(rows(core_recv, 64 * q, 64), co_r.at[q], co_s.at[q], {"tp": sibling})
        both = gu[span(128 * q + c * 64, 64), :] + core_recv[64 * q : 64 * q + 64, :]
        own_sum[64 * q : 64 * q + 64, :] = both
        x_send[64 * q : 64 * q + 64, :] = both.astype(BF16)
        for d in (2, 1, 3):
            to = x_peer(d)
            send(
                rows(x_send, 64 * q + to * 16, 16), rows(x_recv, 64 * q + x * 16, 16),
                xx_s.at[q, d], xx_r.at[q, d], {"tp": to * 2 + c},
            )

    def hidden(q):
        total = own_sum[span(64 * q + x * 16, 16), :]
        for d in range(1, NX):
            src = x_peer(NX - d)
            arrive(rows(x_recv, 64 * q + src * 16, 16), xx_r.at[q, d], xx_s.at[q, d], {"tp": src * 2 + c})
            total += x_recv[span(64 * q + src * 16, 16), :].astype(F32)
        gv, uv = total[:, 0:512], total[:, 512:1024]
        hid = gv / (1.0 + jnp.exp(-gv)) * uv
        place = 128 * q + c * 64 + x * 16
        h_all[span(place, 16), :] = hid.astype(BF16)
        for d in (4, 5, 3, 2, 6, 1, 7):
            send(
                rows(h_all, place, 16), rows(h_all, place, 16), hh_s.at[q, d], hh_r.at[q, d], {"tp": tp_peer(d)}
            )

    def second_ffn(q):
        if q == 0:
            loads[6].wait()
        for d in range(1, 8):
            src = tp_peer(8 - d)
            arrive(
                rows(h_all, 128 * q + src % 2 * 64 + src // 2 * 16, 16),
                hh_r.at[q, d], hh_s.at[q, d], {"tp": tp_peer(d)},
            )
        r_buf[128 * q : 128 * q + 128, :] = dot(h_all[128 * q : 128 * q + 128, :], v_down[...]).astype(BF16)
        for d in (2, 1, 3):
            to = y_peer(d)
            send(
                rows(r_buf, 128 * q + to * 32, 32), rows(p_buf, 128 * q + y * 32, 32),
                yr_s.at[q, d], yr_r.at[q, d], at_dp(z, to),
            )
        p_buf[span(128 * q + y * 32, 32), :] = r_buf[span(128 * q + y * 32, 32), :]

    def combine(q):
        for d in range(1, NY):
            arrive(rows(p_buf, 128 * q + y_peer(NY - d) * 32, 32), yr_r.at[q, d], yr_s.at[q, d], at_dp(z, y_peer(d)))
        meta = zbuf[64 * q : 64 * q + 64, WD:1024].astype(F32)
        col = iota((64, 128), 1)

        def column(at):
            return jnp.sum(jnp.where(col == at, meta, 0.0), axis=1, keepdims=True)

        base = iota((64, 1), 0) // 16 * 8 - 1
        s0, s1 = column(e0).astype(I32), column(e0 + 1).astype(I32)
        t0 = jnp.where(s0 > 0, s0 + base, -1)
        t1 = jnp.where(s1 > 0, s1 + base, -1)
        target = jnp.where(col < 64, t0, t1)
        gate = jnp.where(col < 64, column(e0 + 32), column(e0 + 33))
        mix = jnp.where(col % 32 == target, gate, 0.0).astype(BF16)
        part = dot(mix, p_buf[128 * q : 128 * q + 128, :])
        if q == 0:
            zs0[...] = part
            return
        zs[64 * q : 64 * q + 64, :] = part.astype(BF16)
        for d, at, there, size, i in passing:
            if there // 64 == q:
                dst = {64: rows(ra, 0, 64), 128: rows(rb, 0, 64), 192: rows(rc, 0, 32), 224: rows(rc, 32, 32)}[there]
                send(rows(zs, there, size), dst, rs_s.at[i], rs_r.at[i], z_peer(NZ - d))

    def gather():
        for (d, at, there, size, i), dst in zip(
            passing, (rows(ra, 0, 64), rows(rb, 0, 64), rows(rc, 0, 32), rows(rc, 32, 32))
        ):
            arrive(dst, rs_r.at[i], rs_s.at[i], z_peer(d))
        zs0[...] = zs0[...] + ra[...].astype(F32) + rb[...].astype(F32)
        zs0[0:32, :] = zs0[0:32, :] + rc[0:32, :].astype(F32)
        zs0[16:48, :] = zs0[16:48, :] + rc[32:64, :].astype(F32)
        far_send[...] = zs0[...].astype(BF16)
        for i, d in enumerate((8, 4, 12)):
            send(rows(far_send, 16 * ORDER.index(d), 16), rows(far_recv, 16 * i, 16), rs_s.at[i], rs_r.at[i], z_peer(d))

    def finish_moe():
        total = zs0[16:32, :]
        for i, d in enumerate((8, 4, 12)):
            arrive(rows(far_recv, 16 * i, 16), rs_r.at[i], rs_s.at[i], z_peer(d))
            total += far_recv[16 * i : 16 * i + 16, :].astype(F32)
        moe_out[...] = total.astype(BF16)

    def pack_pages():
        slot = page_slot[...]
        target, position = slot // 32, slot % 32
        r16 = iota((64, 32), 0)
        sel = jnp.where(r16 == 0, (position + 1).astype(F32), jnp.where(r16 == 1, prefill_scale[...].astype(F32), 0.0))
        spread = (iota((256, 32), 0) // 8 == iota((256, 32), 1)).astype(BF16)
        page_tail[:, 64:128] = dot(spread, sel.astype(BF16), 1, 1).astype(BF16)
        wide = jnp.broadcast_to(target.astype(F32), (16, 32)).astype(BF16)
        goal = dot(wide, spread, 1, 1)[0:1].astype(I32) * 8 + iota((1, 256), 1) % 8
        put = jnp.where(iota((512, 256), 0) == goal, 1.0, 0.0).astype(BF16)
        loads[1].wait()
        page_tail[:, 0:64] = v_pages[:, 512:576]
        pg_send[:, 0:512] = dot(put, v_pages[:, 0:512]).astype(BF16)
        pg_send[:, 512:640] = dot(put, page_tail[...]).astype(BF16)

    def send_pages(g):
        for k in range(4 * g, 4 * g + 4):
            d = (NZ - PAGE_ORDER[k]) % NZ
            to = lax.rem(z + d, NZ)
            if d:
                send(rows(pg_send, to * 32, 32), rows(pg_recv, 32 * k, 32), pz_s.at[k], pz_r.at[k], z_peer(d))
            else:
                pg_recv[32 * k : 32 * k + 32, :] = pg_send[span(to * 32, 32), :]

    def turn_pages(g):
        for k in range(4 * g, 4 * g + 4):
            if PAGE_ORDER[k]:
                arrive(rows(pg_recv, 32 * k, 32), pz_r.at[k], pz_s.at[k], z_peer(1))
        r = iota((128, 128), 0)
        src = r % 32 // 8 * 32 + r // 32 * 8 + r % 8
        turn = jnp.where(iota((128, 128), 1) == src, 1.0, 0.0).astype(BF16)
        pg_turn[128 * g : 128 * g + 128, :] = dot(turn, pg_recv[128 * g : 128 * g + 128, :]).astype(BF16)
        for d in (2, 1, 3):
            to = y_peer(d)
            send(
                rows(pg_turn, 128 * g + to * 32, 32), rows(pg_slots, 128 * g + y * 32, 32),
                py_s.at[g, d], py_r.at[g, d], at_dp(z, to),
            )
        pg_slots[span(128 * g + y * 32, 32), :] = pg_turn[span(128 * g + y * 32, 32), :]

    def place_pages():
        for g in range(4):
            for d in range(1, NY):
                src = y_peer(NY - d)
                arrive(rows(pg_slots, 128 * g + src * 32, 32), py_r.at[g, d], py_s.at[g, d], at_dp(z, src))
        pick = (iota((16, 128), 1) == 64).astype(BF16)
        position = dot(pick, pg_slots[:, 512:640], 1, 1)[0:1].astype(I32)
        goal = jnp.where(position > 0, (position - 1) * 8 + iota((1, 512), 1) % 8, -1)
        take = jnp.where(iota((256, 512), 0) == goal, 1.0, 0.0).astype(BF16)
        new_k[...] = dot(take, pg_slots[...]).astype(BF16)

    def score(r):
        if r == 0:
            loads[2].wait()
            loads[3].wait()
        pair, n = r // 2, r % 2
        if r < 2:
            rest = v_res[128 * r : 128 * r + 128, 512:576]
            value = v_res[128 * r : 128 * r + 128, 0:512]
            wide = jnp.broadcast_to(resident_scale[...].astype(F32), (16, 32)).astype(BF16)
            spread = (iota((128, 32), 0) // 8 + 16 * r == iota((128, 32), 1)).astype(BF16)
            scale = dot(spread, wide, 1, 1)[:, 0:1]
        else:
            rest = new_k[128 * n : 128 * n + 128, 512:576]
            value = new_k[128 * n : 128 * n + 128, 0:512]
            scale = new_k[128 * n : 128 * n + 128, 512:640].astype(F32)[:, 65:66]
        s = dot(value, v_q[r, 0:512, :]) + dot(rest, v_q[r, 512:576, :])
        row = iota((128, 128), 0)
        seen = row // 8 * 64 + tp * 8 + row % 8 < lengths[r]
        s = jnp.where(seen, s * (scale * FACTOR), MASKED)
        m = jnp.max(s, axis=0, keepdims=True)
        e = jnp.where(seen, jnp.exp(s - m), 0.0)
        l = jnp.sum(e, axis=0, keepdims=True)
        w = e * (scale / jnp.maximum(l, 1.0))
        part = dot(w.T.astype(BF16), value).astype(BF16)
        for i in range(8):
            at_send[256 * pair + 32 * i + 16 * n : 256 * pair + 32 * i + 16 * n + 16, :] = part[16 * i : 16 * i + 16, :]
        place = span(64 * pair + tp * 8, 8)
        row8 = iota((8, 128), 0)
        rest8 = jnp.zeros((8, 128), F32) if n == 0 else ml[place, :]
        ml[place, :] = jnp.where(row8 == n, m, jnp.where(row8 == n + 4, l, rest8))

    def send_attention(pair):
        for d in (4, 5, 3, 2, 6, 1, 7):
            to = tp_peer(d)
            place = rows(ml, 64 * pair + tp * 8, 8)
            send(place, place, ml_s.at[pair, d], ml_r.at[pair, d], {"tp": to})
            send(
                rows(at_send, 256 * pair + to * 32, 32), rows(at_recv, 256 * pair + tp * 32, 32),
                at_s.at[pair, d], at_r.at[pair, d], {"tp": to},
            )
        at_recv[span(256 * pair + tp * 32, 32), :] = at_send[span(256 * pair + tp * 32, 32), :]

    def finish_attention(pair):
        for d in range(1, 8):
            src = tp_peer(8 - d)
            arrive(rows(ml, 64 * pair + src * 8, 8), ml_r.at[pair, d], ml_s.at[pair, d], {"tp": src})
        m = [ml[64 * pair + 8 * i : 64 * pair + 8 * i + 4, :] for i in range(8)]
        l = [ml[64 * pair + 8 * i + 4 : 64 * pair + 8 * i + 8, :] for i in range(8)]
        highest = m[0]
        for i in range(1, 8):
            highest = jnp.maximum(highest, m[i])
        share = [l[i] * jnp.exp(m[i] - highest) for i in range(8)]
        total = share[0]
        for i in range(1, 8):
            total = total + share[i]
        inverse = 1.0 / total
        stacked = jnp.concatenate([share[i] * inverse for i in range(8)] + [jnp.zeros((96, 128), F32)], axis=0)
        wcol[...] = stacked.T
        mine = wcol[span(tp * 16, 16), :]
        for d in range(1, 8):
            src = tp_peer(8 - d)
            arrive(rows(at_recv, 256 * pair + src * 32, 32), at_r.at[pair, d], at_s.at[pair, d], {"tp": src})
        for n in range(2):
            out = jnp.zeros((16, 512), F32)
            for i in range(8):
                part = at_recv[256 * pair + 32 * i + 16 * n : 256 * pair + 32 * i + 16 * n + 16, :].astype(F32)
                out += part * mine[:, 4 * i + n : 4 * i + n + 1]
            att_out[2 * pair + n] = out.astype(BF16)

    stages = dict(
        enter=enter, far=far, far_wait=far_wait, near=near, near_wait=near_wait, dispatch=dispatch, first=first_ffn,
        over_x=over_x, hidden=hidden, second=second_ffn, combine=combine, gather=gather, finish_moe=finish_moe,
        pack=pack_pages, send_pages=send_pages, turn=turn_pages, place=place_pages, score=score,
        send_att=send_attention, finish_att=finish_attention,
    )
    for line in SCHEDULE:
        name, _, number = line.partition(" ")
        stages[name](*([int(number)] if number else []))
    for copy in started:
        copy.wait_send()


def on_device(
    queries, lengths, resident_pages, resident_scale, prefill_written_pages, prefill_scale,
    page_slot, tokens, expert_ids, gate_weights, gate_projection, up_weights, down_weights,
):
    vmem = pl.BlockSpec(memory_space=pltpu.VMEM)
    smem = pl.BlockSpec(memory_space=pltpu.SMEM)
    hbm = pl.BlockSpec(memory_space=pl.ANY)
    dma = pltpu.SemaphoreType.DMA
    return pl.pallas_call(
        kernel,
        out_shape=(
            jax.ShapeDtypeStruct((4, 16, 512), BF16),
            jax.ShapeDtypeStruct((16, WD), BF16),
        ),
        in_specs=[hbm, smem, hbm, vmem, hbm, vmem, vmem, hbm, vmem, vmem, hbm, hbm, hbm],
        out_specs=(vmem, vmem),
        scratch_shapes=[
            pltpu.VMEM((WD, 512), BF16),
            pltpu.VMEM((WD, 512), BF16),
            pltpu.VMEM((512, WD), BF16),
            pltpu.VMEM((4, 576, 128), BF16),
            pltpu.VMEM((256, 576), BF16),
            pltpu.VMEM((256, 576), BF16),
            pltpu.VMEM((256, 1024), BF16),
            pltpu.VMEM((256, WD), BF16),
            pltpu.VMEM((512, WD), BF16),
            pltpu.VMEM((512, 1024), F32),
            pltpu.VMEM((256, 1024), F32),
            pltpu.VMEM((256, 1024), F32),
            pltpu.VMEM((256, 1024), BF16),
            pltpu.VMEM((256, 1024), BF16),
            pltpu.VMEM((512, 512), BF16),
            pltpu.VMEM((512, WD), BF16),
            pltpu.VMEM((512, WD), BF16),
            pltpu.VMEM((64, WD), F32),
            pltpu.VMEM((256, WD), BF16),
            pltpu.VMEM((64, WD), BF16),
            pltpu.VMEM((64, WD), BF16),
            pltpu.VMEM((64, WD), BF16),
            pltpu.VMEM((64, WD), BF16),
            pltpu.VMEM((48, WD), BF16),
            pltpu.VMEM((256, 1024), F32),
            pltpu.VMEM((256, 128), BF16),
            pltpu.VMEM((512, 640), BF16),
            pltpu.VMEM((512, 640), BF16),
            pltpu.VMEM((512, 640), BF16),
            pltpu.VMEM((512, 640), BF16),
            pltpu.VMEM((256, 640), BF16),
            pltpu.VMEM((128, 128), F32),
            pltpu.VMEM((512, 512), BF16),
            pltpu.VMEM((512, 512), BF16),
            pltpu.VMEM((128, 128), F32),
            dma((7,)),
            dma((7,)), dma((7,)),
            dma((QN, 4)), dma((QN, 4)),
            dma((QN,)), dma((QN,)),
            dma((QN, 4)), dma((QN, 4)),
            dma((QN, 8)), dma((QN, 8)),
            dma((QN, 4)), dma((QN, 4)),
            dma((7,)), dma((7,)),
            dma((16,)), dma((16,)),
            dma((4, 4)), dma((4, 4)),
            dma((2, 8)), dma((2, 8)),
            dma((2, 8)), dma((2, 8)),
        ],
        compiler_params=pltpu.CompilerParams(
            collective_id=0, has_side_effects=True, vmem_limit_bytes=60 * 1024 * 1024
        ),
    )(
        queries.transpose(0, 2, 1),
        lengths,
        resident_pages.reshape(256, 576),
        resident_scale.reshape(1, 32),
        prefill_written_pages.reshape(256, 576),
        prefill_scale.reshape(1, 32),
        page_slot.reshape(1, 32),
        tokens,
        expert_ids.T,
        gate_weights.T,
        gate_projection.reshape(WD, 512),
        up_weights.reshape(WD, 512),
        down_weights.reshape(512, WD),
    )


def solution(mesh):
    placed = (
        P("dp", None, None), P("dp"), P("dp", "tp", None), P("dp"), P("dp", "tp", None), P("dp"),
        P("dp"), P("dp", None), P("dp", None), P("dp", None), P("dp", "tp", None),
        P("dp", "tp", None), P("dp", None, "tp"),
    )
    return jax.shard_map(
        on_device, mesh=mesh, in_specs=placed, out_specs=(P("dp", "tp", None), P("dp", "tp")),
        check_vma=False,
    )
```

```python
import jax
import jax.numpy as jnp
from jax import lax
from jax.experimental import pallas as pl
from jax.experimental.pallas import tpu as pltpu
from jax.sharding import PartitionSpec as P

F32, BF16, I32 = jnp.float32, jnp.bfloat16, jnp.int32
MESH = pl.DeviceIdType.MESH
FACTOR = 192.0 ** (-0.5)
MASKED = -1e30
SCHEDULE = [
    "pack", "score 0", "score 1", "enter", "far", "send_att 0", "far_wait", "near", "dispatch 0",
    "near_wait 1", "dispatch 1", "first 0", "near_wait 2", "dispatch 2", "over_x 0", "near_wait 3", "dispatch 3",
    "send_pages 0", "send_pages 1", "send_pages 2", "send_pages 3", "first 1", "hidden 0", "over_x 1", "first 2",
    "second 0", "hidden 1", "over_x 2", "first 3", "second 1", "hidden 2", "over_x 3", "combine 0", "second 2",
    "hidden 3", "combine 1", "turn 0", "second 3", "combine 2", "turn 1", "combine 3", "turn 2", "finish_att 0",
    "turn 3", "place", "gather", "score 2", "score 3", "send_att 1", "finish_moe", "finish_att 1",
]
NZ, NY, NX = 16, 4, 4
QN = 4
WD = 896
ORDER = [12, 0, 4, 8, 13, 1, 5, 9, 11, 15, 3, 7, 10, 14, 2, 6]
PAGE_ORDER = [8, 9, 7, 10, 6, 11, 5, 12, 4, 13, 3, 14, 2, 15, 1, 0]


def dot(a, b, ca=1, cb=0):
    return lax.dot_general(a, b, (((ca,), (cb,)), ((), ())), preferred_element_type=F32)


def iota(shape, dim):
    return lax.broadcasted_iota(I32, shape, dim)


def kernel(
    queries, lengths, resident, resident_scale, pages, prefill_scale, page_slot,
    tokens, ids, gates, gate_w, up_w, down_w,
    att_out, moe_out,
    v_gate, v_up, v_down, v_q, v_res, v_pages, zbuf, dsend, ffn_x, gu, core_send, core_recv, x_send, x_recv,
    h_all, r_buf, p_buf, zs0, zs, ra, rb, rc, far_send, far_recv, own_sum,
    page_tail, pg_send, pg_recv, tl_send, tl_recv, pg_turn, pg_slots, new_k, ml, at_send, at_recv, wcol,
    load_sem, zg_s, zg_r, yd_s, yd_r, co_s, co_r, xx_s, xx_r, hh_s, hh_r,
    yr_s, yr_r, rs_s, rs_r, pz_s, pz_r, pt_s, pt_r, py_s, py_r, ml_s, ml_r, at_s, at_r,
):
    tp = lax.axis_index("tp")
    dp = lax.axis_index("dp")
    x, c = tp // 2, tp % 2
    z, y = dp // NY, dp % NY

    def at_dp(zz, yy):
        return {"dp": zz * NY + yy}

    def z_peer(d):
        return at_dp(lax.rem(z + d, NZ), y)

    def y_peer(d):
        return lax.rem(y + d, NY)

    def tp_peer(d):
        return lax.rem(tp + d, 8)

    def x_peer(d):
        return lax.rem(x + d, NX)

    sibling = x * 2 + (1 - c)

    def span(start, size):
        if not isinstance(start, int):
            start = pl.multiple_of(start, 8 if size % 16 else 16)
        return pl.ds(start, size)

    def rows(ref, start, size):
        return ref.at[span(start, size), :]

    started = []

    def remote(src, dst, ssem, rsem, where):
        return pltpu.make_async_remote_copy(
            src_ref=src, dst_ref=dst, send_sem=ssem, recv_sem=rsem,
            device_id=where, device_id_type=MESH,
        )

    def send(src, dst, ssem, rsem, where):
        copy = remote(src, dst, ssem, rsem, where)
        copy.start()
        started.append(copy)

    def arrive(dst, rsem, ssem, where):
        remote(dst, dst, ssem, rsem, where).wait_recv()

    barrier = pltpu.get_barrier_semaphore()
    for d in range(1, NZ):
        pl.semaphore_signal(barrier, inc=1, device_id=z_peer(d), device_id_type=MESH)
    for d in range(1, NY):
        pl.semaphore_signal(barrier, inc=1, device_id=at_dp(z, y_peer(d)), device_id_type=MESH)
    for d in range(1, 8):
        pl.semaphore_signal(barrier, inc=1, device_id={"tp": tp_peer(d)}, device_id_type=MESH)

    local = [
        (tokens.at[:, pl.ds(pl.multiple_of(tp * WD, 128), WD)], zbuf.at[pl.ds(16, 16), pl.ds(0, WD)]),
        (pages, v_pages),
        (resident, v_res),
        (queries, v_q),
        (gate_w, v_gate),
        (up_w, v_up),
        (down_w, v_down),
    ]
    loads = [pltpu.make_async_copy(src, dst, load_sem.at[i]) for i, (src, dst) in enumerate(local)]
    for copy in loads:
        copy.start()

    lane = iota((16, 128), 1)
    idv = ids[...].astype(F32).T.astype(I32)
    gwv = gates[...].astype(F32).T
    chosen = jnp.zeros((16, 128), F32)
    gate_l = jnp.zeros((16, 128), F32)
    for k in range(8):
        chosen += jnp.where(idv[:, k : k + 1] == lane, 1.0, 0.0)
        gate_l += jnp.where(idv[:, k : k + 1] + 32 == lane, gwv[:, k : k + 1], 0.0)
    before = (iota((16, 16), 1) < iota((16, 16), 0)).astype(BF16)
    rank = dot(before, chosen.astype(BF16))
    slot = page_slot[...]
    r16 = iota((16, 32), 0)
    sel = jnp.where(r16 == 0, (slot % 32 + 1).astype(F32), jnp.where(r16 == 1, prefill_scale[...].astype(F32), 0.0))
    goes = (iota((128, 32), 0) - 64 == slot // 32).astype(BF16)
    page_meta = dot(sel.astype(BF16), goes, 1, 1)
    zbuf[16:32, WD:1024] = (chosen * (rank + 1.0) + gate_l + page_meta).astype(BF16)

    def enter():
        loads[0].wait()
        pl.semaphore_wait(barrier, NZ - 1 + NY - 1 + 7)

    def far():
        for i, d in enumerate((8, 4, 12)):
            send(rows(zbuf, 16, 16), rows(zbuf, 16 * ORDER.index(NZ - d), 16), zg_s.at[i], zg_r.at[i], z_peer(d))

    def far_wait():
        for i, d in enumerate((8, 4, 12)):
            arrive(rows(zbuf, 16 * ORDER.index(NZ - d), 16), zg_r.at[i], zg_s.at[i], z_peer(d))

    passing = [(NZ - 1, 0, 64, 64, 3), (1, 0, 128, 64, 4), (2, 0, 192, 32, 5), (NZ - 2, 16, 224, 32, 6)]

    def near():
        for d, at, there, size, i in passing:
            send(rows(zbuf, at, size), rows(zbuf, there, size), zg_s.at[i], zg_r.at[i], z_peer(d))

    def near_wait(q):
        for d, at, there, size, i in passing:
            if there // 64 == q:
                arrive(rows(zbuf, there, size), zg_r.at[i], zg_s.at[i], z_peer(d))

    e0 = 2 * z

    def dispatch(q):
        meta = zbuf[64 * q : 64 * q + 64, WD:1024]
        pick = (iota((16, 128), 1) == e0 + iota((16, 128), 0)).astype(BF16)
        slots = dot(pick, meta, 1, 1).astype(I32)
        base = iota((1, 64), 1) // 16 * 8 - 1
        t0 = jnp.where(slots[0:1] > 0, slots[0:1] + base, -1)
        t1 = jnp.where(slots[1:2] > 0, slots[1:2] + base + 32, -1)
        row = iota((64, 64), 0)
        g = jnp.where(row == jnp.where(row < 32, t0, t1), 1.0, 0.0).astype(BF16)
        dsend[64 * q : 64 * q + 64, :] = dot(g, zbuf[64 * q : 64 * q + 64, 0:WD]).astype(BF16)
        for d in (2, 1, 3):
            to = y_peer(d)
            send(
                rows(dsend, 64 * q + to // 2 * 32, 32), rows(ffn_x, 128 * q + y * 32, 32),
                yd_s.at[q, d], yd_r.at[q, d], at_dp(z, to),
            )
        ffn_x[span(128 * q + y * 32, 32), :] = dsend[span(64 * q + y // 2 * 32, 32), :]

    def first_ffn(q):
        if q == 0:
            loads[4].wait()
            loads[5].wait()
        for d in range(1, NY):
            arrive(rows(ffn_x, 128 * q + y_peer(NY - d) * 32, 32), yd_r.at[q, d], yd_s.at[q, d], at_dp(z, y_peer(d)))
        a = ffn_x[128 * q : 128 * q + 128, :]
        gu[128 * q : 128 * q + 128, 0:512] = dot(a, v_gate[...])
        gu[128 * q : 128 * q + 128, 512:1024] = dot(a, v_up[...])
        core_send[64 * q : 64 * q + 64, :] = gu[span(128 * q + (1 - c) * 64, 64), :]
        send(
            rows(core_send, 64 * q, 64), rows(core_recv, 64 * q, 64), co_s.at[q], co_r.at[q], {"tp": sibling}
        )

    def over_x(q):
        arrive(rows(core_recv, 64 * q, 64), co_r.at[q], co_s.at[q], {"tp": sibling})
        both = gu[span(128 * q + c * 64, 64), :] + core_recv[64 * q : 64 * q + 64, :]
        own_sum[64 * q : 64 * q + 64, :] = both
        x_send[64 * q : 64 * q + 64, :] = both.astype(BF16)
        for d in (2, 1, 3):
            to = x_peer(d)
            send(
                rows(x_send, 64 * q + to * 16, 16), rows(x_recv, 64 * q + x * 16, 16),
                xx_s.at[q, d], xx_r.at[q, d], {"tp": to * 2 + c},
            )

    def hidden(q):
        total = own_sum[span(64 * q + x * 16, 16), :]
        for d in range(1, NX):
            src = x_peer(NX - d)
            arrive(rows(x_recv, 64 * q + src * 16, 16), xx_r.at[q, d], xx_s.at[q, d], {"tp": src * 2 + c})
            total += x_recv[span(64 * q + src * 16, 16), :].astype(F32)
        gv, uv = total[:, 0:512], total[:, 512:1024]
        hid = gv / (1.0 + jnp.exp(-gv)) * uv
        place = 128 * q + c * 64 + x * 16
        h_all[span(place, 16), :] = hid.astype(BF16)
        for d in (4, 5, 3, 2, 6, 1, 7):
            send(
                rows(h_all, place, 16), rows(h_all, place, 16), hh_s.at[q, d], hh_r.at[q, d], {"tp": tp_peer(d)}
            )

    def second_ffn(q):
        if q == 0:
            loads[6].wait()
        for d in range(1, 8):
            src = tp_peer(8 - d)
            arrive(
                rows(h_all, 128 * q + src % 2 * 64 + src // 2 * 16, 16),
                hh_r.at[q, d], hh_s.at[q, d], {"tp": tp_peer(d)},
            )
        r_buf[128 * q : 128 * q + 128, :] = dot(h_all[128 * q : 128 * q + 128, :], v_down[...]).astype(BF16)
        for d in (2, 1, 3):
            to = y_peer(d)
            send(
                rows(r_buf, 128 * q + to * 32, 32), rows(p_buf, 128 * q + y * 32, 32),
                yr_s.at[q, d], yr_r.at[q, d], at_dp(z, to),
            )
        p_buf[span(128 * q + y * 32, 32), :] = r_buf[span(128 * q + y * 32, 32), :]

    def combine(q):
        for d in range(1, NY):
            arrive(rows(p_buf, 128 * q + y_peer(NY - d) * 32, 32), yr_r.at[q, d], yr_s.at[q, d], at_dp(z, y_peer(d)))
        meta = zbuf[64 * q : 64 * q + 64, WD:1024].astype(F32)
        col = iota((64, 128), 1)

        def column(at):
            return jnp.sum(jnp.where(col == at, meta, 0.0), axis=1, keepdims=True)

        base = iota((64, 1), 0) // 16 * 8 - 1
        s0, s1 = column(e0).astype(I32), column(e0 + 1).astype(I32)
        t0 = jnp.where(s0 > 0, s0 + base, -1)
        t1 = jnp.where(s1 > 0, s1 + base, -1)
        target = jnp.where(col < 64, t0, t1)
        gate = jnp.where(col < 64, column(e0 + 32), column(e0 + 33))
        mix = jnp.where(col % 32 == target, gate, 0.0).astype(BF16)
        part = dot(mix, p_buf[128 * q : 128 * q + 128, :])
        if q == 0:
            zs0[...] = part
            return
        zs[64 * q : 64 * q + 64, :] = part.astype(BF16)
        for d, at, there, size, i in passing:
            if there // 64 == q:
                dst = {64: rows(ra, 0, 64), 128: rows(rb, 0, 64), 192: rows(rc, 0, 32), 224: rows(rc, 32, 32)}[there]
                send(rows(zs, there, size), dst, rs_s.at[i], rs_r.at[i], z_peer(NZ - d))

    def gather():
        for (d, at, there, size, i), dst in zip(
            passing, (rows(ra, 0, 64), rows(rb, 0, 64), rows(rc, 0, 32), rows(rc, 32, 32))
        ):
            arrive(dst, rs_r.at[i], rs_s.at[i], z_peer(d))
        zs0[...] = zs0[...] + ra[...].astype(F32) + rb[...].astype(F32)
        zs0[0:32, :] = zs0[0:32, :] + rc[0:32, :].astype(F32)
        zs0[16:48, :] = zs0[16:48, :] + rc[32:64, :].astype(F32)
        far_send[...] = zs0[...].astype(BF16)
        for i, d in enumerate((8, 4, 12)):
            send(rows(far_send, 16 * ORDER.index(d), 16), rows(far_recv, 16 * i, 16), rs_s.at[i], rs_r.at[i], z_peer(d))

    def finish_moe():
        total = zs0[16:32, :]
        for i, d in enumerate((8, 4, 12)):
            arrive(rows(far_recv, 16 * i, 16), rs_r.at[i], rs_s.at[i], z_peer(d))
            total += far_recv[16 * i : 16 * i + 16, :].astype(F32)
        moe_out[...] = total.astype(BF16)

    def pack_pages():
        spread = (iota((256, 32), 0) // 8 == iota((256, 32), 1)).astype(BF16)
        wide = jnp.broadcast_to((slot // 32).astype(F32), (16, 32)).astype(BF16)
        goal = dot(wide, spread, 1, 1)[0:1].astype(I32) * 8 + iota((1, 256), 1) % 8
        put = jnp.where(iota((512, 256), 0) == goal, 1.0, 0.0).astype(BF16)
        loads[1].wait()
        pg_send[...] = dot(put, v_pages[:, 0:512]).astype(BF16)
        page_tail[0, :, 0:64] = v_pages[:, 512:576]
        page_tail[0, :, 64:128] = jnp.zeros((256, 64), BF16)
        page_tail[1, :, 0:64] = jnp.zeros((256, 64), BF16)
        page_tail[1, :, 64:128] = v_pages[:, 512:576]
        row = iota((256, 256), 0)
        first = row // 16 * 32 + row % 16
        low = jnp.where(first == goal, 1.0, 0.0).astype(BF16)
        high = jnp.where(first + 16 == goal, 1.0, 0.0).astype(BF16)
        tl_send[...] = (dot(low, page_tail[0]) + dot(high, page_tail[1])).astype(BF16)

    def send_pages(g):
        for k in range(4 * g, 4 * g + 4):
            d = (NZ - PAGE_ORDER[k]) % NZ
            to = lax.rem(z + d, NZ)
            if d:
                send(rows(pg_send, to * 32, 32), rows(pg_recv, 32 * k, 32), pz_s.at[k], pz_r.at[k], z_peer(d))
                send(rows(tl_send, to * 16, 16), rows(tl_recv, 16 * k, 16), pt_s.at[k], pt_r.at[k], z_peer(d))
            else:
                pg_recv[32 * k : 32 * k + 32, :] = pg_send[span(to * 32, 32), :]
                tl_recv[16 * k : 16 * k + 16, :] = tl_send[span(to * 16, 16), :]

    def turn_pages(g):
        for k in range(4 * g, 4 * g + 4):
            if PAGE_ORDER[k]:
                arrive(rows(pg_recv, 32 * k, 32), pz_r.at[k], pz_s.at[k], z_peer(1))
                arrive(rows(tl_recv, 16 * k, 16), pt_r.at[k], pt_s.at[k], z_peer(1))
        r = iota((128, 128), 0)
        src = r % 32 // 8 * 32 + r // 32 * 8 + r % 8
        turn = jnp.where(iota((128, 128), 1) == src, 1.0, 0.0).astype(BF16)
        pg_turn[128 * g : 128 * g + 128, 0:512] = dot(turn, pg_recv[128 * g : 128 * g + 128, :]).astype(BF16)
        r = iota((128, 64), 0)
        src = r % 32 // 8 * 16 + r // 32 % 2 * 8 + r % 8
        turn = jnp.where(iota((128, 64), 1) == src, 1.0, 0.0).astype(BF16)
        tail = dot(turn, tl_recv[64 * g : 64 * g + 64, :])
        swapped = jnp.concatenate([tail[:, 64:128], tail[:, 0:64]], axis=1)
        r, lane = iota((128, 128), 0), iota((128, 128), 1)
        place, scale = jnp.zeros((128, 128), F32), jnp.zeros((128, 128), F32)
        for k in range(4):
            at = 16 * ORDER.index(PAGE_ORDER[4 * g + k])
            meta = zbuf[at : at + 16, WD:1024].astype(F32)
            place = jnp.where(r % 32 // 8 == k, meta[0:1], place)
            scale = jnp.where(r % 32 // 8 == k, meta[1:2], scale)
        hit = lane == 64 + 4 * z + r // 32
        place = jnp.sum(jnp.where(hit, place, 0.0), axis=1, keepdims=True)
        scale = jnp.sum(jnp.where(hit, scale, 0.0), axis=1, keepdims=True)
        tail = jnp.where(lane < 64, jnp.where(r < 64, tail, swapped), 0.0)
        tail = jnp.where(lane == 64, place, jnp.where(lane == 65, scale, tail))
        pg_turn[128 * g : 128 * g + 128, 512:640] = tail.astype(BF16)
        for d in (2, 1, 3):
            to = y_peer(d)
            send(
                rows(pg_turn, 128 * g + to * 32, 32), rows(pg_slots, 128 * g + y * 32, 32),
                py_s.at[g, d], py_r.at[g, d], at_dp(z, to),
            )
        pg_slots[span(128 * g + y * 32, 32), :] = pg_turn[span(128 * g + y * 32, 32), :]

    def place_pages():
        for g in range(4):
            for d in range(1, NY):
                src = y_peer(NY - d)
                arrive(rows(pg_slots, 128 * g + src * 32, 32), py_r.at[g, d], py_s.at[g, d], at_dp(z, src))
        pick = (iota((16, 128), 1) == 64).astype(BF16)
        position = dot(pick, pg_slots[:, 512:640], 1, 1)[0:1].astype(I32)
        goal = jnp.where(position > 0, (position - 1) * 8 + iota((1, 512), 1) % 8, -1)
        take = jnp.where(iota((256, 512), 0) == goal, 1.0, 0.0).astype(BF16)
        new_k[...] = dot(take, pg_slots[...]).astype(BF16)

    def score(r):
        if r == 0:
            loads[2].wait()
            loads[3].wait()
        pair, n = r // 2, r % 2
        if r < 2:
            rest = v_res[128 * r : 128 * r + 128, 512:576]
            value = v_res[128 * r : 128 * r + 128, 0:512]
            wide = jnp.broadcast_to(resident_scale[...].astype(F32), (16, 32)).astype(BF16)
            spread = (iota((128, 32), 0) // 8 + 16 * r == iota((128, 32), 1)).astype(BF16)
            scale = dot(spread, wide, 1, 1)[:, 0:1]
        else:
            rest = new_k[128 * n : 128 * n + 128, 512:576]
            value = new_k[128 * n : 128 * n + 128, 0:512]
            scale = new_k[128 * n : 128 * n + 128, 512:640].astype(F32)[:, 65:66]
        s = dot(value, v_q[r, 0:512, :]) + dot(rest, v_q[r, 512:576, :])
        row = iota((128, 128), 0)
        seen = row // 8 * 64 + tp * 8 + row % 8 < lengths[r]
        s = jnp.where(seen, s * (scale * FACTOR), MASKED)
        m = jnp.max(s, axis=0, keepdims=True)
        e = jnp.where(seen, jnp.exp(s - m), 0.0)
        l = jnp.sum(e, axis=0, keepdims=True)
        w = e * (scale / jnp.maximum(l, 1.0))
        part = dot(w.T.astype(BF16), value).astype(BF16)
        for i in range(8):
            at_send[256 * pair + 32 * i + 16 * n : 256 * pair + 32 * i + 16 * n + 16, :] = part[16 * i : 16 * i + 16, :]
        place = span(64 * pair + tp * 8, 8)
        row8 = iota((8, 128), 0)
        rest8 = jnp.zeros((8, 128), F32) if n == 0 else ml[place, :]
        ml[place, :] = jnp.where(row8 == n, m, jnp.where(row8 == n + 4, l, rest8))

    def send_attention(pair):
        for d in (4, 5, 3, 2, 6, 1, 7):
            to = tp_peer(d)
            place = rows(ml, 64 * pair + tp * 8, 8)
            send(place, place, ml_s.at[pair, d], ml_r.at[pair, d], {"tp": to})
            send(
                rows(at_send, 256 * pair + to * 32, 32), rows(at_recv, 256 * pair + tp * 32, 32),
                at_s.at[pair, d], at_r.at[pair, d], {"tp": to},
            )
        at_recv[span(256 * pair + tp * 32, 32), :] = at_send[span(256 * pair + tp * 32, 32), :]

    def finish_attention(pair):
        for d in range(1, 8):
            src = tp_peer(8 - d)
            arrive(rows(ml, 64 * pair + src * 8, 8), ml_r.at[pair, d], ml_s.at[pair, d], {"tp": src})
        m = [ml[64 * pair + 8 * i : 64 * pair + 8 * i + 4, :] for i in range(8)]
        l = [ml[64 * pair + 8 * i + 4 : 64 * pair + 8 * i + 8, :] for i in range(8)]
        highest = m[0]
        for i in range(1, 8):
            highest = jnp.maximum(highest, m[i])
        share = [l[i] * jnp.exp(m[i] - highest) for i in range(8)]
        total = share[0]
        for i in range(1, 8):
            total = total + share[i]
        inverse = 1.0 / total
        stacked = jnp.concatenate([share[i] * inverse for i in range(8)] + [jnp.zeros((96, 128), F32)], axis=0)
        wcol[...] = stacked.T
        mine = wcol[span(tp * 16, 16), :]
        for d in range(1, 8):
            src = tp_peer(8 - d)
            arrive(rows(at_recv, 256 * pair + src * 32, 32), at_r.at[pair, d], at_s.at[pair, d], {"tp": src})
        for n in range(2):
            out = jnp.zeros((16, 512), F32)
            for i in range(8):
                part = at_recv[256 * pair + 32 * i + 16 * n : 256 * pair + 32 * i + 16 * n + 16, :].astype(F32)
                out += part * mine[:, 4 * i + n : 4 * i + n + 1]
            att_out[2 * pair + n] = out.astype(BF16)

    stages = dict(
        enter=enter, far=far, far_wait=far_wait, near=near, near_wait=near_wait, dispatch=dispatch, first=first_ffn,
        over_x=over_x, hidden=hidden, second=second_ffn, combine=combine, gather=gather, finish_moe=finish_moe,
        pack=pack_pages, send_pages=send_pages, turn=turn_pages, place=place_pages, score=score,
        send_att=send_attention, finish_att=finish_attention,
    )
    for line in SCHEDULE:
        name, _, number = line.partition(" ")
        stages[name](*([int(number)] if number else []))
    for copy in started:
        copy.wait_send()


def on_device(
    queries, lengths, resident_pages, resident_scale, prefill_written_pages, prefill_scale,
    page_slot, tokens, expert_ids, gate_weights, gate_projection, up_weights, down_weights,
):
    vmem = pl.BlockSpec(memory_space=pltpu.VMEM)
    smem = pl.BlockSpec(memory_space=pltpu.SMEM)
    hbm = pl.BlockSpec(memory_space=pl.ANY)
    dma = pltpu.SemaphoreType.DMA
    return pl.pallas_call(
        kernel,
        out_shape=(
            jax.ShapeDtypeStruct((4, 16, 512), BF16),
            jax.ShapeDtypeStruct((16, WD), BF16),
        ),
        in_specs=[hbm, smem, hbm, vmem, hbm, vmem, vmem, hbm, vmem, vmem, hbm, hbm, hbm],
        out_specs=(vmem, vmem),
        scratch_shapes=[
            pltpu.VMEM((WD, 512), BF16),
            pltpu.VMEM((WD, 512), BF16),
            pltpu.VMEM((512, WD), BF16),
            pltpu.VMEM((4, 576, 128), BF16),
            pltpu.VMEM((256, 576), BF16),
            pltpu.VMEM((256, 576), BF16),
            pltpu.VMEM((256, 1024), BF16),
            pltpu.VMEM((256, WD), BF16),
            pltpu.VMEM((512, WD), BF16),
            pltpu.VMEM((512, 1024), F32),
            pltpu.VMEM((256, 1024), F32),
            pltpu.VMEM((256, 1024), F32),
            pltpu.VMEM((256, 1024), BF16),
            pltpu.VMEM((256, 1024), BF16),
            pltpu.VMEM((512, 512), BF16),
            pltpu.VMEM((512, WD), BF16),
            pltpu.VMEM((512, WD), BF16),
            pltpu.VMEM((64, WD), F32),
            pltpu.VMEM((256, WD), BF16),
            pltpu.VMEM((64, WD), BF16),
            pltpu.VMEM((64, WD), BF16),
            pltpu.VMEM((64, WD), BF16),
            pltpu.VMEM((64, WD), BF16),
            pltpu.VMEM((48, WD), BF16),
            pltpu.VMEM((256, 1024), F32),
            pltpu.VMEM((2, 256, 128), BF16),
            pltpu.VMEM((512, 512), BF16),
            pltpu.VMEM((512, 512), BF16),
            pltpu.VMEM((256, 128), BF16),
            pltpu.VMEM((256, 128), BF16),
            pltpu.VMEM((512, 640), BF16),
            pltpu.VMEM((512, 640), BF16),
            pltpu.VMEM((256, 640), BF16),
            pltpu.VMEM((128, 128), F32),
            pltpu.VMEM((512, 512), BF16),
            pltpu.VMEM((512, 512), BF16),
            pltpu.VMEM((128, 128), F32),
            dma((7,)),
            dma((7,)), dma((7,)),
            dma((QN, 4)), dma((QN, 4)),
            dma((QN,)), dma((QN,)),
            dma((QN, 4)), dma((QN, 4)),
            dma((QN, 8)), dma((QN, 8)),
            dma((QN, 4)), dma((QN, 4)),
            dma((7,)), dma((7,)),
            dma((16,)), dma((16,)),
            dma((16,)), dma((16,)),
            dma((4, 4)), dma((4, 4)),
            dma((2, 8)), dma((2, 8)),
            dma((2, 8)), dma((2, 8)),
        ],
        compiler_params=pltpu.CompilerParams(
            collective_id=0, has_side_effects=True, vmem_limit_bytes=60 * 1024 * 1024
        ),
    )(
        queries.transpose(0, 2, 1),
        lengths,
        resident_pages.reshape(256, 576),
        resident_scale.reshape(1, 32),
        prefill_written_pages.reshape(256, 576),
        prefill_scale.reshape(1, 32),
        page_slot.reshape(1, 32),
        tokens,
        expert_ids.T,
        gate_weights.T,
        gate_projection.reshape(WD, 512),
        up_weights.reshape(WD, 512),
        down_weights.reshape(512, WD),
    )


def solution(mesh):
    placed = (
        P("dp", None, None), P("dp"), P("dp", "tp", None), P("dp"), P("dp", "tp", None), P("dp"),
        P("dp"), P("dp", None), P("dp", None), P("dp", None), P("dp", "tp", None),
        P("dp", "tp", None), P("dp", None, "tp"),
    )
    return jax.shard_map(
        on_device, mesh=mesh, in_specs=placed, out_specs=(P("dp", "tp", None), P("dp", "tp")),
        check_vma=False,
    )
```

```python
import jax
import jax.numpy as jnp
from jax import lax
from jax.experimental import pallas as pl
from jax.experimental.pallas import tpu as pltpu
from jax.sharding import PartitionSpec as P

F32, BF16, I32 = jnp.float32, jnp.bfloat16, jnp.int32
MESH = pl.DeviceIdType.MESH
FACTOR = 192.0 ** (-0.5)
MASKED = -1e30
SCHEDULE = [
    "pack", "score 0", "score 1", "enter", "far", "pages_y", "send_att 0", "far_wait", "near", "dispatch 0",
    "near_wait 1", "dispatch 1", "first 0", "near_wait 2", "dispatch 2", "over_x 0", "near_wait 3", "dispatch 3",
    "turn", "send_pages 0", "send_pages 1", "send_pages 2", "send_pages 3", "first 1", "hidden 0", "over_x 1", "first 2",
    "second 0", "hidden 1", "over_x 2", "first 3", "second 1", "hidden 2", "over_x 3", "combine 0", "second 2",
    "hidden 3", "combine 1", "second 3", "combine 2", "combine 3", "finish_att 0", "unpack 0", "unpack 1", "unpack 2",
    "unpack 3", "place", "score 2", "score 3", "send_att 1", "gather", "finish_att 1", "finish_moe",
]
NZ, NY, NX = 16, 4, 4
QN = 4
WD = 896
ORDER = [12, 0, 4, 8, 13, 1, 5, 9, 11, 15, 3, 7, 10, 14, 2, 6]
PAGE_ORDER = [8, 9, 7, 10, 6, 11, 5, 12, 4, 13, 3, 14, 2, 15, 1, 0]


def dot(a, b, ca=1, cb=0):
    return lax.dot_general(a, b, (((ca,), (cb,)), ((), ())), preferred_element_type=F32)


def iota(shape, dim):
    return lax.broadcasted_iota(I32, shape, dim)


def kernel(
    queries, lengths, resident, resident_scale, pages, prefill_scale, page_slot,
    tokens, ids, gates, gate_w, up_w, down_w,
    att_out, moe_out,
    v_gate, v_up, v_down, v_q, v_res, v_pages, zbuf, dsend, ffn_x, gu, core_send, core_recv, x_send, x_recv,
    h_all, r_buf, p_buf, zs0, zs, ra, rb, rc, far_send, far_recv, own_sum,
    page_tail, pg_send, pg_y, pg_z, tl_z, mt_z, tl_recv, mt_recv, pg_slots, new_k, ml, at_send, at_recv, wcol,
    load_sem, zg_s, zg_r, yd_s, yd_r, co_s, co_r, xx_s, xx_r, hh_s, hh_r,
    yr_s, yr_r, rs_s, rs_r, pz_s, pz_r, pt_s, pt_r, pm_s, pm_r, py_s, py_r, ml_s, ml_r, at_s, at_r,
):
    tp = lax.axis_index("tp")
    dp = lax.axis_index("dp")
    x, c = tp // 2, tp % 2
    z, y = dp // NY, dp % NY

    def at_dp(zz, yy):
        return {"dp": zz * NY + yy}

    def z_peer(d):
        return at_dp(lax.rem(z + d, NZ), y)

    def y_peer(d):
        return lax.rem(y + d, NY)

    def tp_peer(d):
        return lax.rem(tp + d, 8)

    def x_peer(d):
        return lax.rem(x + d, NX)

    sibling = x * 2 + (1 - c)

    def span(start, size):
        if not isinstance(start, int):
            start = pl.multiple_of(start, 8 if size % 16 else 16)
        return pl.ds(start, size)

    def rows(ref, start, size):
        return ref.at[span(start, size), :]

    started = []

    def remote(src, dst, ssem, rsem, where):
        return pltpu.make_async_remote_copy(
            src_ref=src, dst_ref=dst, send_sem=ssem, recv_sem=rsem,
            device_id=where, device_id_type=MESH,
        )

    def send(src, dst, ssem, rsem, where):
        copy = remote(src, dst, ssem, rsem, where)
        copy.start()
        started.append(copy)

    def arrive(dst, rsem, ssem, where):
        remote(dst, dst, ssem, rsem, where).wait_recv()

    barrier = pltpu.get_barrier_semaphore()
    for d in range(1, NZ):
        pl.semaphore_signal(barrier, inc=1, device_id=z_peer(d), device_id_type=MESH)
    for d in range(1, NY):
        pl.semaphore_signal(barrier, inc=1, device_id=at_dp(z, y_peer(d)), device_id_type=MESH)
    for d in range(1, 8):
        pl.semaphore_signal(barrier, inc=1, device_id={"tp": tp_peer(d)}, device_id_type=MESH)

    local = [
        (tokens.at[:, pl.ds(pl.multiple_of(tp * WD, 128), WD)], zbuf.at[pl.ds(16, 16), pl.ds(0, WD)]),
        (pages, v_pages),
        (resident, v_res),
        (queries, v_q),
        (gate_w, v_gate),
        (up_w, v_up),
        (down_w, v_down),
    ]
    loads = [pltpu.make_async_copy(src, dst, load_sem.at[i]) for i, (src, dst) in enumerate(local)]
    for copy in loads:
        copy.start()

    lane = iota((16, 128), 1)
    idv = ids[...].astype(F32).T.astype(I32)
    gwv = gates[...].astype(F32).T
    chosen = jnp.zeros((16, 128), F32)
    gate_l = jnp.zeros((16, 128), F32)
    for k in range(8):
        chosen += jnp.where(idv[:, k : k + 1] == lane, 1.0, 0.0)
        gate_l += jnp.where(idv[:, k : k + 1] + 32 == lane, gwv[:, k : k + 1], 0.0)
    before = (iota((16, 16), 1) < iota((16, 16), 0)).astype(BF16)
    rank = dot(before, chosen.astype(BF16))
    zbuf[16:32, WD:1024] = (chosen * (rank + 1.0) + gate_l).astype(BF16)

    def enter():
        loads[0].wait()
        pl.semaphore_wait(barrier, NZ - 1 + NY - 1 + 7)

    def far():
        for i, d in enumerate((8, 4, 12)):
            send(rows(zbuf, 16, 16), rows(zbuf, 16 * ORDER.index(NZ - d), 16), zg_s.at[i], zg_r.at[i], z_peer(d))

    def far_wait():
        for i, d in enumerate((8, 4, 12)):
            arrive(rows(zbuf, 16 * ORDER.index(NZ - d), 16), zg_r.at[i], zg_s.at[i], z_peer(d))

    passing = [(NZ - 1, 0, 64, 64, 3), (1, 0, 128, 64, 4), (2, 0, 192, 32, 5), (NZ - 2, 16, 224, 32, 6)]

    def near():
        for d, at, there, size, i in passing:
            send(rows(zbuf, at, size), rows(zbuf, there, size), zg_s.at[i], zg_r.at[i], z_peer(d))

    def near_wait(q):
        for d, at, there, size, i in passing:
            if there // 64 == q:
                arrive(rows(zbuf, there, size), zg_r.at[i], zg_s.at[i], z_peer(d))

    e0 = 2 * z

    def dispatch(q):
        meta = zbuf[64 * q : 64 * q + 64, WD:1024]
        pick = (iota((16, 128), 1) == e0 + iota((16, 128), 0)).astype(BF16)
        slots = dot(pick, meta, 1, 1).astype(I32)
        base = iota((1, 64), 1) // 16 * 8 - 1
        t0 = jnp.where(slots[0:1] > 0, slots[0:1] + base, -1)
        t1 = jnp.where(slots[1:2] > 0, slots[1:2] + base + 32, -1)
        row = iota((64, 64), 0)
        g = jnp.where(row == jnp.where(row < 32, t0, t1), 1.0, 0.0).astype(BF16)
        dsend[64 * q : 64 * q + 64, :] = dot(g, zbuf[64 * q : 64 * q + 64, 0:WD]).astype(BF16)
        for d in (2, 1, 3):
            to = y_peer(d)
            send(
                rows(dsend, 64 * q + to // 2 * 32, 32), rows(ffn_x, 128 * q + y * 32, 32),
                yd_s.at[q, d], yd_r.at[q, d], at_dp(z, to),
            )
        ffn_x[span(128 * q + y * 32, 32), :] = dsend[span(64 * q + y // 2 * 32, 32), :]

    def first_ffn(q):
        if q == 0:
            loads[4].wait()
            loads[5].wait()
        for d in range(1, NY):
            arrive(rows(ffn_x, 128 * q + y_peer(NY - d) * 32, 32), yd_r.at[q, d], yd_s.at[q, d], at_dp(z, y_peer(d)))
        a = ffn_x[128 * q : 128 * q + 128, :]
        gu[128 * q : 128 * q + 128, 0:512] = dot(a, v_gate[...])
        gu[128 * q : 128 * q + 128, 512:1024] = dot(a, v_up[...])
        core_send[64 * q : 64 * q + 64, :] = gu[span(128 * q + (1 - c) * 64, 64), :]
        send(
            rows(core_send, 64 * q, 64), rows(core_recv, 64 * q, 64), co_s.at[q], co_r.at[q], {"tp": sibling}
        )

    def over_x(q):
        arrive(rows(core_recv, 64 * q, 64), co_r.at[q], co_s.at[q], {"tp": sibling})
        both = gu[span(128 * q + c * 64, 64), :] + core_recv[64 * q : 64 * q + 64, :]
        own_sum[64 * q : 64 * q + 64, :] = both
        x_send[64 * q : 64 * q + 64, :] = both.astype(BF16)
        for d in (2, 1, 3):
            to = x_peer(d)
            send(
                rows(x_send, 64 * q + to * 16, 16), rows(x_recv, 64 * q + x * 16, 16),
                xx_s.at[q, d], xx_r.at[q, d], {"tp": to * 2 + c},
            )

    def hidden(q):
        total = own_sum[span(64 * q + x * 16, 16), :]
        for d in range(1, NX):
            src = x_peer(NX - d)
            arrive(rows(x_recv, 64 * q + src * 16, 16), xx_r.at[q, d], xx_s.at[q, d], {"tp": src * 2 + c})
            total += x_recv[span(64 * q + src * 16, 16), :].astype(F32)
        gv, uv = total[:, 0:512], total[:, 512:1024]
        hid = gv / (1.0 + jnp.exp(-gv)) * uv
        place = 128 * q + c * 64 + x * 16
        h_all[span(place, 16), :] = hid.astype(BF16)
        for d in (4, 5, 3, 2, 6, 1, 7):
            send(
                rows(h_all, place, 16), rows(h_all, place, 16), hh_s.at[q, d], hh_r.at[q, d], {"tp": tp_peer(d)}
            )

    def second_ffn(q):
        if q == 0:
            loads[6].wait()
        for d in range(1, 8):
            src = tp_peer(8 - d)
            arrive(
                rows(h_all, 128 * q + src % 2 * 64 + src // 2 * 16, 16),
                hh_r.at[q, d], hh_s.at[q, d], {"tp": tp_peer(d)},
            )
        r_buf[128 * q : 128 * q + 128, :] = dot(h_all[128 * q : 128 * q + 128, :], v_down[...]).astype(BF16)
        for d in (2, 1, 3):
            to = y_peer(d)
            send(
                rows(r_buf, 128 * q + to * 32, 32), rows(p_buf, 128 * q + y * 32, 32),
                yr_s.at[q, d], yr_r.at[q, d], at_dp(z, to),
            )
        p_buf[span(128 * q + y * 32, 32), :] = r_buf[span(128 * q + y * 32, 32), :]

    def combine(q):
        for d in range(1, NY):
            arrive(rows(p_buf, 128 * q + y_peer(NY - d) * 32, 32), yr_r.at[q, d], yr_s.at[q, d], at_dp(z, y_peer(d)))
        meta = zbuf[64 * q : 64 * q + 64, WD:1024].astype(F32)
        col = iota((64, 128), 1)

        def column(at):
            return jnp.sum(jnp.where(col == at, meta, 0.0), axis=1, keepdims=True)

        base = iota((64, 1), 0) // 16 * 8 - 1
        s0, s1 = column(e0).astype(I32), column(e0 + 1).astype(I32)
        t0 = jnp.where(s0 > 0, s0 + base, -1)
        t1 = jnp.where(s1 > 0, s1 + base, -1)
        target = jnp.where(col < 64, t0, t1)
        gate = jnp.where(col < 64, column(e0 + 32), column(e0 + 33))
        mix = jnp.where(col % 32 == target, gate, 0.0).astype(BF16)
        part = dot(mix, p_buf[128 * q : 128 * q + 128, :])
        if q == 0:
            zs0[...] = part
            return
        zs[64 * q : 64 * q + 64, :] = part.astype(BF16)
        for d, at, there, size, i in passing:
            if there // 64 == q:
                dst = {64: rows(ra, 0, 64), 128: rows(rb, 0, 64), 192: rows(rc, 0, 32), 224: rows(rc, 32, 32)}[there]
                send(rows(zs, there, size), dst, rs_s.at[i], rs_r.at[i], z_peer(NZ - d))

    def gather():
        for (d, at, there, size, i), dst in zip(
            passing, (rows(ra, 0, 64), rows(rb, 0, 64), rows(rc, 0, 32), rows(rc, 32, 32))
        ):
            arrive(dst, rs_r.at[i], rs_s.at[i], z_peer(d))
        zs0[...] = zs0[...] + ra[...].astype(F32) + rb[...].astype(F32)
        zs0[0:32, :] = zs0[0:32, :] + rc[0:32, :].astype(F32)
        zs0[16:48, :] = zs0[16:48, :] + rc[32:64, :].astype(F32)
        far_send[...] = zs0[...].astype(BF16)
        for i, d in enumerate((8, 4, 12)):
            send(rows(far_send, 16 * ORDER.index(d), 16), rows(far_recv, 16 * i, 16), rs_s.at[i], rs_r.at[i], z_peer(d))

    def finish_moe():
        total = zs0[16:32, :]
        for i, d in enumerate((8, 4, 12)):
            arrive(rows(far_recv, 16 * i, 16), rs_r.at[i], rs_s.at[i], z_peer(d))
            total += far_recv[16 * i : 16 * i + 16, :].astype(F32)
        moe_out[...] = total.astype(BF16)

    def pack_pages():
        slot = page_slot[...]
        r64 = iota((64, 32), 0)
        sel = jnp.where(
            r64 == 0, (slot % 32 + 1).astype(F32), jnp.where(r64 == 1, prefill_scale[...].astype(F32), 0.0)
        )
        spread = (iota((256, 32), 0) // 8 == iota((256, 32), 1)).astype(BF16)
        page_tail[:, 64:128] = dot(spread, sel.astype(BF16), 1, 1).astype(BF16)
        target = slot // 32
        where = target % 4 * 16 + target // 4
        wide = jnp.broadcast_to(where.astype(F32), (16, 32)).astype(BF16)
        goal = dot(wide, spread, 1, 1)[0:1].astype(I32) * 8 + iota((1, 256), 1) % 8
        put = jnp.where(iota((512, 256), 0) == goal, 1.0, 0.0).astype(BF16)
        loads[1].wait()
        page_tail[:, 0:64] = v_pages[:, 512:576]
        pg_send[:, 0:512] = dot(put, v_pages[:, 0:512]).astype(BF16)
        pg_send[:, 512:640] = dot(put, page_tail[...]).astype(BF16)

    def pages_y():
        for d in (2, 1, 3):
            to = y_peer(d)
            send(rows(pg_send, to * 128, 128), rows(pg_y, y * 128, 128), py_s.at[d], py_r.at[d], at_dp(z, to))
        pg_y[span(y * 128, 128), :] = pg_send[span(y * 128, 128), :]

    def turn_pages():
        for d in range(1, NY):
            arrive(rows(pg_y, y_peer(NY - d) * 128, 128), py_r.at[d], py_s.at[d], at_dp(z, y_peer(d)))
        r, col = iota((512, 512), 0), iota((512, 512), 1)
        turn = jnp.where(col == r % 32 // 8 * 128 + r // 32 * 8 + r % 8, 1.0, 0.0).astype(BF16)
        pg_z[...] = dot(turn, pg_y[:, 0:512]).astype(BF16)
        tail = pg_y[:, 512:640]
        lane = iota((512, 128), 1)
        columns = jnp.where(lane < 64, tail.astype(F32), 0.0)
        swapped = jnp.concatenate([columns[:, 64:128], columns[:, 0:64]], axis=1)
        r, col = iota((256, 512), 0), iota((256, 512), 1)
        src = r % 16 // 8 * 128 + r // 16 * 8 + r % 8
        low = jnp.where(col == src, 1.0, 0.0).astype(BF16)
        high = jnp.where(col == src + 256, 1.0, 0.0).astype(BF16)
        tl_z[...] = (dot(low, columns.astype(BF16)) + dot(high, swapped.astype(BF16))).astype(BF16)
        r, lane, col = iota((16, 128), 0), iota((16, 128), 1), iota((16, 512), 1)
        meta = jnp.zeros((16, 128), F32)
        for k in range(4):
            first = jnp.where(col == k * 128 + iota((16, 512), 0) * 8, 1.0, 0.0).astype(BF16)
            got = dot(first, tail)
            meta = jnp.where(lane == k, got[:, 64:65], jnp.where(lane == k + 8, got[:, 65:66], meta))
        for k in range(NZ):
            mt_z[k] = meta[k : k + 1, :]

    def send_pages(g):
        for k in range(4 * g, 4 * g + 4):
            d = (NZ - PAGE_ORDER[k]) % NZ
            to = lax.rem(z + d, NZ)
            if d:
                send(rows(pg_z, to * 32, 32), pg_slots.at[pl.ds(32 * k, 32), pl.ds(0, 512)], pz_s.at[k], pz_r.at[k], z_peer(d))
                send(rows(tl_z, to * 16, 16), rows(tl_recv, 16 * k, 16), pt_s.at[k], pt_r.at[k], z_peer(d))
                send(mt_z.at[to], mt_recv.at[k], pm_s.at[k], pm_r.at[k], z_peer(d))
            else:
                pg_slots[32 * k : 32 * k + 32, 0:512] = pg_z[span(to * 32, 32), :]
                tl_recv[16 * k : 16 * k + 16, :] = tl_z[span(to * 16, 16), :]
                mt_recv[k] = mt_z[to]

    def unpack(g):
        for k in range(4 * g, 4 * g + 4):
            if PAGE_ORDER[k]:
                arrive(pg_slots.at[pl.ds(32 * k, 32), pl.ds(0, 512)], pz_r.at[k], pz_s.at[k], z_peer(1))
                arrive(rows(tl_recv, 16 * k, 16), pt_r.at[k], pt_s.at[k], z_peer(1))
                arrive(mt_recv.at[k], pm_r.at[k], pm_s.at[k], z_peer(1))
        r, col = iota((128, 64), 0), iota((128, 64), 1)
        pick = jnp.where(col == r // 32 * 16 + r % 16, 1.0, 0.0).astype(BF16)
        tail = dot(pick, tl_recv[64 * g : 64 * g + 64, :])
        swapped = jnp.concatenate([tail[:, 64:128], tail[:, 0:64]], axis=1)
        r, lane = iota((128, 128), 0), iota((128, 128), 1)
        meta = jnp.zeros((128, 128), F32)
        for k in range(4):
            meta = jnp.where(r // 32 == k, mt_recv[4 * g + k], meta)
        place = jnp.sum(jnp.where(lane == r % 32 // 8, meta, 0.0), axis=1, keepdims=True)
        scale = jnp.sum(jnp.where(lane == r % 32 // 8 + 8, meta, 0.0), axis=1, keepdims=True)
        tail = jnp.where(lane < 64, jnp.where(r % 32 < 16, tail, swapped), 0.0)
        tail = jnp.where(lane == 64, place, jnp.where(lane == 65, scale, tail))
        pg_slots[128 * g : 128 * g + 128, 512:640] = tail.astype(BF16)

    def place_pages():
        pick = (iota((16, 128), 1) == 64).astype(BF16)
        position = dot(pick, pg_slots[:, 512:640], 1, 1)[0:1].astype(I32)
        goal = jnp.where(position > 0, (position - 1) * 8 + iota((1, 512), 1) % 8, -1)
        take = jnp.where(iota((256, 512), 0) == goal, 1.0, 0.0).astype(BF16)
        new_k[...] = dot(take, pg_slots[...]).astype(BF16)

    def score(r):
        if r == 0:
            loads[2].wait()
            loads[3].wait()
        pair, n = r // 2, r % 2
        if r < 2:
            rest = v_res[128 * r : 128 * r + 128, 512:576]
            value = v_res[128 * r : 128 * r + 128, 0:512]
            wide = jnp.broadcast_to(resident_scale[...].astype(F32), (16, 32)).astype(BF16)
            spread = (iota((128, 32), 0) // 8 + 16 * r == iota((128, 32), 1)).astype(BF16)
            scale = dot(spread, wide, 1, 1)[:, 0:1]
        else:
            rest = new_k[128 * n : 128 * n + 128, 512:576]
            value = new_k[128 * n : 128 * n + 128, 0:512]
            scale = new_k[128 * n : 128 * n + 128, 512:640].astype(F32)[:, 65:66]
        s = dot(value, v_q[r, 0:512, :]) + dot(rest, v_q[r, 512:576, :])
        row = iota((128, 128), 0)
        seen = row // 8 * 64 + tp * 8 + row % 8 < lengths[r]
        s = jnp.where(seen, s * (scale * FACTOR), MASKED)
        m = jnp.max(s, axis=0, keepdims=True)
        e = jnp.where(seen, jnp.exp(s - m), 0.0)
        l = jnp.sum(e, axis=0, keepdims=True)
        w = e * (scale / jnp.maximum(l, 1.0))
        part = dot(w.T.astype(BF16), value).astype(BF16)
        for i in range(8):
            at_send[256 * pair + 32 * i + 16 * n : 256 * pair + 32 * i + 16 * n + 16, :] = part[16 * i : 16 * i + 16, :]
        place = span(64 * pair + tp * 8, 8)
        row8 = iota((8, 128), 0)
        rest8 = jnp.zeros((8, 128), F32) if n == 0 else ml[place, :]
        ml[place, :] = jnp.where(row8 == n, m, jnp.where(row8 == n + 4, l, rest8))

    def send_attention(pair):
        for d in (4, 5, 3, 2, 6, 1, 7):
            to = tp_peer(d)
            place = rows(ml, 64 * pair + tp * 8, 8)
            send(place, place, ml_s.at[pair, d], ml_r.at[pair, d], {"tp": to})
            send(
                rows(at_send, 256 * pair + to * 32, 32), rows(at_recv, 256 * pair + tp * 32, 32),
                at_s.at[pair, d], at_r.at[pair, d], {"tp": to},
            )
        at_recv[span(256 * pair + tp * 32, 32), :] = at_send[span(256 * pair + tp * 32, 32), :]

    def finish_attention(pair):
        for d in range(1, 8):
            src = tp_peer(8 - d)
            arrive(rows(ml, 64 * pair + src * 8, 8), ml_r.at[pair, d], ml_s.at[pair, d], {"tp": src})
        m = [ml[64 * pair + 8 * i : 64 * pair + 8 * i + 4, :] for i in range(8)]
        l = [ml[64 * pair + 8 * i + 4 : 64 * pair + 8 * i + 8, :] for i in range(8)]
        highest = m[0]
        for i in range(1, 8):
            highest = jnp.maximum(highest, m[i])
        share = [l[i] * jnp.exp(m[i] - highest) for i in range(8)]
        total = share[0]
        for i in range(1, 8):
            total = total + share[i]
        inverse = 1.0 / total
        stacked = jnp.concatenate([share[i] * inverse for i in range(8)] + [jnp.zeros((96, 128), F32)], axis=0)
        wcol[...] = stacked.T
        mine = wcol[span(tp * 16, 16), :]
        for d in range(1, 8):
            src = tp_peer(8 - d)
            arrive(rows(at_recv, 256 * pair + src * 32, 32), at_r.at[pair, d], at_s.at[pair, d], {"tp": src})
        for n in range(2):
            out = jnp.zeros((16, 512), F32)
            for i in range(8):
                part = at_recv[256 * pair + 32 * i + 16 * n : 256 * pair + 32 * i + 16 * n + 16, :].astype(F32)
                out += part * mine[:, 4 * i + n : 4 * i + n + 1]
            att_out[2 * pair + n] = out.astype(BF16)

    stages = dict(
        enter=enter, far=far, far_wait=far_wait, near=near, near_wait=near_wait, dispatch=dispatch, first=first_ffn,
        over_x=over_x, hidden=hidden, second=second_ffn, combine=combine, gather=gather, finish_moe=finish_moe,
        pack=pack_pages, send_pages=send_pages, pages_y=pages_y, turn=turn_pages, unpack=unpack, place=place_pages, score=score,
        send_att=send_attention, finish_att=finish_attention,
    )
    for line in SCHEDULE:
        name, _, number = line.partition(" ")
        stages[name](*([int(number)] if number else []))
    for copy in started:
        copy.wait_send()


def on_device(
    queries, lengths, resident_pages, resident_scale, prefill_written_pages, prefill_scale,
    page_slot, tokens, expert_ids, gate_weights, gate_projection, up_weights, down_weights,
):
    vmem = pl.BlockSpec(memory_space=pltpu.VMEM)
    smem = pl.BlockSpec(memory_space=pltpu.SMEM)
    hbm = pl.BlockSpec(memory_space=pl.ANY)
    dma = pltpu.SemaphoreType.DMA
    return pl.pallas_call(
        kernel,
        out_shape=(
            jax.ShapeDtypeStruct((4, 16, 512), BF16),
            jax.ShapeDtypeStruct((16, WD), BF16),
        ),
        in_specs=[hbm, smem, hbm, vmem, hbm, vmem, vmem, hbm, vmem, vmem, hbm, hbm, hbm],
        out_specs=(vmem, vmem),
        scratch_shapes=[
            pltpu.VMEM((WD, 512), BF16),
            pltpu.VMEM((WD, 512), BF16),
            pltpu.VMEM((512, WD), BF16),
            pltpu.VMEM((4, 576, 128), BF16),
            pltpu.VMEM((256, 576), BF16),
            pltpu.VMEM((256, 576), BF16),
            pltpu.VMEM((256, 1024), BF16),
            pltpu.VMEM((256, WD), BF16),
            pltpu.VMEM((512, WD), BF16),
            pltpu.VMEM((512, 1024), F32),
            pltpu.VMEM((256, 1024), F32),
            pltpu.VMEM((256, 1024), F32),
            pltpu.VMEM((256, 1024), BF16),
            pltpu.VMEM((256, 1024), BF16),
            pltpu.VMEM((512, 512), BF16),
            pltpu.VMEM((512, WD), BF16),
            pltpu.VMEM((512, WD), BF16),
            pltpu.VMEM((64, WD), F32),
            pltpu.VMEM((256, WD), BF16),
            pltpu.VMEM((64, WD), BF16),
            pltpu.VMEM((64, WD), BF16),
            pltpu.VMEM((64, WD), BF16),
            pltpu.VMEM((64, WD), BF16),
            pltpu.VMEM((48, WD), BF16),
            pltpu.VMEM((256, 1024), F32),
            pltpu.VMEM((256, 128), BF16),
            pltpu.VMEM((512, 640), BF16),
            pltpu.VMEM((512, 640), BF16),
            pltpu.VMEM((512, 512), BF16),
            pltpu.VMEM((256, 128), BF16),
            pltpu.VMEM((16, 1, 128), F32),
            pltpu.VMEM((256, 128), BF16),
            pltpu.VMEM((16, 1, 128), F32),
            pltpu.VMEM((512, 640), BF16),
            pltpu.VMEM((256, 640), BF16),
            pltpu.VMEM((128, 128), F32),
            pltpu.VMEM((512, 512), BF16),
            pltpu.VMEM((512, 512), BF16),
            pltpu.VMEM((128, 128), F32),
            dma((7,)),
            dma((7,)), dma((7,)),
            dma((QN, 4)), dma((QN, 4)),
            dma((QN,)), dma((QN,)),
            dma((QN, 4)), dma((QN, 4)),
            dma((QN, 8)), dma((QN, 8)),
            dma((QN, 4)), dma((QN, 4)),
            dma((7,)), dma((7,)),
            dma((16,)), dma((16,)),
            dma((16,)), dma((16,)),
            dma((16,)), dma((16,)),
            dma((4,)), dma((4,)),
            dma((2, 8)), dma((2, 8)),
            dma((2, 8)), dma((2, 8)),
        ],
        compiler_params=pltpu.CompilerParams(
            collective_id=0, has_side_effects=True, vmem_limit_bytes=60 * 1024 * 1024
        ),
    )(
        queries.transpose(0, 2, 1),
        lengths,
        resident_pages.reshape(256, 576),
        resident_scale.reshape(1, 32),
        prefill_written_pages.reshape(256, 576),
        prefill_scale.reshape(1, 32),
        page_slot.reshape(1, 32),
        tokens,
        expert_ids.T,
        gate_weights.T,
        gate_projection.reshape(WD, 512),
        up_weights.reshape(WD, 512),
        down_weights.reshape(512, WD),
    )


def solution(mesh):
    placed = (
        P("dp", None, None), P("dp"), P("dp", "tp", None), P("dp"), P("dp", "tp", None), P("dp"),
        P("dp"), P("dp", None), P("dp", None), P("dp", None), P("dp", "tp", None),
        P("dp", "tp", None), P("dp", None, "tp"),
    )
    return jax.shard_map(
        on_device, mesh=mesh, in_specs=placed, out_specs=(P("dp", "tp", None), P("dp", "tp")),
        check_vma=False,
    )
```
